256 devices in a mesh: aux: 4 (over y), mu: 4 (over z_lo, core), nu: 16 (over x, z_hi).
Axes of the slice: x: 4, y: 4, z: 8 (z_hi: 4, z_lo: 2; z = z_hi * 2 + z_lo), core: 2. Of those that a mesh axis runs over, the one named last changes fastest.
Arguments:
- integrals: bfloat16 [256, 1024, 1024], P('aux', 'nu', 'mu'), may hold values from -0.625 to 0.625
- integral_mask: int32 [4, 16, 16], P('aux', 'nu', 'mu'), may hold values 0 or 1
- density: bfloat16 [1024, 1024], P('mu', 'nu'), as said below
- density_mask: int32 [16, 16], P('mu', 'nu'), may hold values from 0 to 1, as said below
Outputs:
- exchange_matrix: float32 [1024, 1024], P(('aux', 'mu', 'nu'))
The draws below stay inside these ranges and needn't reach their ends.
Inputs may be any that keep to these rules, and one draw needn't show every extreme that they name: `density`: symmetric. `density_mask`: symmetric, with every diagonal block present and some off-diagonal block absent.
All inputs are finite; a program needn't handle non-finite values. No bound on the sum of `integral_mask` on one device may be relied on, other than what follows from the above.
Results may differ from the reference program's by a relative error of at most 0.0029.
Values may be sent and summed in bfloat16 or wider, within the bound.
No kernel may reach another device: no remote copies, remote signals or barrier semaphores. Data moves between devices by JAX's collectives and lax.ppermute only.
A program may use at most 64 MiB of HBM per device.

```python
import jax
import jax.numpy as jnp
from jax import lax

BW = 64
NB = 16
NA = 1024
NAUX = 256


def draw_density(key, part):
    key = jax.random.fold_in(key, 11)
    values = jax.random.normal(key, (NA, NA), jnp.float32)
    return ((values + values.T) * (0.5 * (2.0 / NA) ** 0.5)).astype(jnp.bfloat16)


def draw_density_mask(key, part):
    key = jax.random.fold_in(key, 17)
    key_values = jax.random.fold_in(key, 1)
    key_first = jax.random.fold_in(key, 2)
    key_step = jax.random.fold_in(key, 3)
    values = jax.random.randint(key_values, (NB, NB), 0, 2)
    row_index = lax.broadcasted_iota(jnp.int32, (NB, NB), 0)
    col_index = lax.broadcasted_iota(jnp.int32, (NB, NB), 1)
    symmetric = jnp.where(row_index <= col_index, values, values.T)
    first = jax.random.randint(key_first, (), 0, NB)
    second = (first + 1 + jax.random.randint(key_step, (), 0, NB - 1)) % NB
    absent = (row_index == first) & (col_index == second) | (row_index == second) & (col_index == first)
    symmetric = jnp.where(absent, 0, symmetric)
    diagonal_ones = (row_index == col_index).astype(jnp.int32)
    return jnp.maximum(symmetric, diagonal_ones).astype(jnp.int32)


def place_ends(array, stream_key, least, top_value):
    longest = array.shape.index(max(array.shape))
    spots = []
    for shift in (0, 1):
        where = [jax.random.randint(jax.random.fold_in(stream_key, axis), (), 0, length) for axis, length in enumerate(array.shape)]
        where[longest] = (where[longest] + shift) % array.shape[longest]
        spots.append(tuple(where))
    return array.at[spots[0]].set(least).at[spots[1]].set(top_value)


def levels(key, extent, pieces, smallest, high):
    def one(dim, parts):
        draws = jax.random.uniform(jax.random.fold_in(jax.random.fold_in(key, 6), dim), (parts,), jnp.float32, smallest / len(pieces), high / len(pieces))
        return jnp.repeat(jnp.exp(draws), extent[dim] // parts).reshape((-1,) + (1,) * (len(extent) - dim - 1))

    factor_of = one(*pieces[0])
    for cut in pieces[1:]:
        factor_of = factor_of * one(*cut)
    return factor_of


def normal_values(stream_key, extent, deviation, reach, pieces=(), kind=jnp.bfloat16):
    entries = jax.random.normal(stream_key, extent, jnp.float32) * deviation
    if len(pieces) > 0:
        entries = levels(stream_key, extent, pieces, -0.22, 0.18) * entries
    return jnp.clip(entries, min=-reach, max=reach).astype(kind)


def setup_inputs(seed: int = 0) -> dict:
    streams_of = jax.random.split(jax.random.key(seed), 5)
    return {
        "integrals": normal_values(streams_of[0], (NAUX, NA, NA), ((NAUX * NA) ** -0.25), 0.625, ((0, 4), (1, 16), (2, 4))),
        "integral_mask": place_ends((jax.random.randint(streams_of[1], (NAUX // BW, NB, NB), 0, 5) < 3).astype(jnp.int32), jax.random.fold_in(streams_of[1], 1), 0, 1),
        "density": draw_density(jax.random.fold_in(streams_of[4], 71), 0),
        "density_mask": draw_density_mask(jax.random.fold_in(streams_of[4], 71), 0),
    }


def expand(blocks, width):
    widened = blocks
    for axis in range(blocks.ndim):
        widened = jnp.repeat(widened, width, axis=axis)
    return widened


def reference(integrals, integral_mask, density, density_mask):
    masked_density = (density * expand(density_mask, BW).astype(jnp.bfloat16)).astype(jnp.float32)
    grouped = integrals.reshape(NAUX // BW, BW, NA, NA)

    def one_group(inputs):
        values, blocks = inputs
        screened = (values * expand(blocks, BW).astype(jnp.bfloat16)).astype(jnp.float32)
        contracted = jnp.einsum("pml,ls->pms", screened, masked_density).astype(jnp.bfloat16)
        contracted = lax.optimization_barrier(contracted).astype(jnp.float32)
        return jnp.einsum("pms,pns->mn", contracted, screened)

    terms = lax.map(one_group, (grouped, integral_mask))
    return jnp.sum(terms, axis=0)
```

```python
import jax
import jax.numpy as jnp
from jax import lax
from jax.experimental import pallas as pl
from jax.experimental.pallas import tpu as pltpu
from jax.sharding import Mesh, PartitionSpec as P

BW = 64
NA = 1024
PLANE = ("x", "c", "zh", "zl")
SPREAD = ("x", "zh", "zl")
OWNERS = ("y", "zl", "x", "zh")
NT = (((1,), (1,)), ((), ()))


def first_kernel(where, parts, mask, *refs):
    mine, theirs = refs[0:4], refs[4:8]
    other_out, own_contracted, screened, density, contracted = refs[8:]
    y, c = where[0], where[1]
    for x in range(4):
        for zh in range(4):
            rows = slice((x * 4 + zh) * BW, (x * 4 + zh + 1) * BW)
            for zl in range(2):
                for core in range(2):
                    cols = slice((zl * 2 + core) * 256, (zl * 2 + core + 1) * 256)
                    block = ((x * 2 + core) * 4 + zh) * 2 + zl
                    screened[rows, cols] = parts[block] * mask[x * 4 + zh, :, cols]
    for step in range(4):
        from_y = lax.rem(y + 4 - step, 4)
        for source, core in ((mine[step], c), (theirs[step], 1 - c)):
            for x in range(4):
                for zh in range(4):
                    row = pl.multiple_of((x * 4 + zh) * BW + from_y * 16, 16)
                    for zl in range(2):
                        col = pl.multiple_of((zl * 2 + core) * 256, 256)
                        density[pl.ds(row, 16), pl.ds(col, 256)] = source[(x * 4 + zh) * 2 + zl]
    for chunk in range(4):
        rows = slice(chunk * 256, (chunk + 1) * 256)
        got = jnp.dot(screened[rows, :], density[...], preferred_element_type=jnp.float32)
        got = got.astype(jnp.bfloat16)
        for zl in range(2):
            for core in range(2):
                low = (zl * 2 + core) * BW
                contracted[lax.rem(core + c, 2), pl.ds((chunk * 2 + zl) * BW, BW), :] = got[low : low + BW]
    own_contracted[...] = contracted[0]
    for half in range(2):
        rows = slice(half * 256, (half + 1) * 256)
        other_out[rows, :] = lax.dot_general(
            contracted[1, rows, :], screened[...], NT, preferred_element_type=jnp.float32
        ).astype(jnp.bfloat16)


def second_kernel(contracted, screened, out):
    for half in range(2):
        rows = slice(half * 256, (half + 1) * 256)
        out[rows, :] = lax.dot_general(
            contracted[rows, :], screened[...], NT, preferred_element_type=jnp.float32
        )


def gather_density(density, density_mask):
    y = lax.axis_index("y")
    wide = jnp.repeat(density_mask[:, 0], BW).astype(jnp.bfloat16)
    block = density.T * wide[None, :]
    piece = lax.dynamic_slice(block, (16 * y, 0), (16, 256))
    plane = lax.all_to_all(
        jnp.broadcast_to(piece[None], (32, 16, 256)), SPREAD, split_axis=0, concat_axis=0, tiled=True
    )
    mine = [plane] + [lax.ppermute(plane, "y", [(i, (i + j) % 4) for i in range(4)]) for j in range(1, 4)]
    theirs = [lax.ppermute(one, "c", [(0, 1), (1, 0)]) for one in mine]
    return mine, theirs


def gather_mask(integral_mask):
    wide = jnp.repeat(integral_mask[0, 0], BW).astype(jnp.bfloat16).reshape(1, 2, 128)
    got = lax.all_to_all(
        jnp.broadcast_to(wide, (64, 2, 128)), PLANE, split_axis=0, concat_axis=0, tiled=True
    )
    got = got.reshape(4, 2, 4, 2, 256).transpose(0, 2, 3, 1, 4)
    return got.reshape(16, 1, NA)


def body(integrals, integral_mask, density, density_mask):
    parts = lax.all_to_all(integrals, PLANE, split_axis=0, concat_axis=0, tiled=True)
    mask = gather_mask(integral_mask)
    mine, theirs = gather_density(density, density_mask)
    where = jnp.stack([lax.axis_index("y"), lax.axis_index("c")]).astype(jnp.int32)
    vmem = pl.BlockSpec(memory_space=pltpu.VMEM)
    smem = pl.BlockSpec(memory_space=pltpu.SMEM)
    half = jax.ShapeDtypeStruct((NA // 2, NA), jnp.bfloat16)
    other_half, own_contracted, screened = pl.pallas_call(
        first_kernel,
        out_shape=(half, half, jax.ShapeDtypeStruct((NA, NA), jnp.bfloat16)),
        in_specs=[smem] + [vmem] * 10,
        out_specs=(vmem, vmem, vmem),
        scratch_shapes=[pltpu.VMEM((NA, NA), jnp.bfloat16), pltpu.VMEM((2, NA // 2, NA), jnp.bfloat16)],
        compiler_params=pltpu.CompilerParams(vmem_limit_bytes=40 * 2**20),
        cost_estimate=pl.CostEstimate(flops=3 * 2**30, bytes_accessed=8 * 2**20, transcendentals=0),
        name="contract",
    )(where, parts, mask, *mine, *theirs)
    arrived = lax.ppermute(other_half, "c", [(0, 1), (1, 0)])
    own_half = pl.pallas_call(
        second_kernel,
        out_shape=jax.ShapeDtypeStruct((NA // 2, NA), jnp.float32),
        in_specs=[vmem] * 2,
        out_specs=vmem,
        compiler_params=pltpu.CompilerParams(vmem_limit_bytes=40 * 2**20),
        cost_estimate=pl.CostEstimate(flops=2**30, bytes_accessed=5 * 2**20, transcendentals=0),
        name="exchange",
    )(own_contracted, screened)
    term = (own_half + arrived.astype(jnp.float32)).astype(jnp.bfloat16).reshape(128, 4, NA)
    terms = lax.all_to_all(term, OWNERS, split_axis=0, concat_axis=0, tiled=True)
    return jnp.sum(terms.astype(jnp.float32), axis=0)


def solution(mesh):
    fine = Mesh(mesh.devices.reshape(4, 2, 2, 4, 4), ("y", "zl", "c", "x", "zh"))
    m, n = ("zl", "c"), ("x", "zh")
    in_specs = (P("y", n, m), P("y", n, m), P(m, n), P(m, n))
    out_specs = P(("y", "zl", "c", "x", "zh"), None)
    return jax.shard_map(body, mesh=fine, in_specs=in_specs, out_specs=out_specs, check_vma=False)
```

```python
import jax
import jax.numpy as jnp
from jax import lax
from jax.experimental import pallas as pl
from jax.experimental.pallas import tpu as pltpu
from jax.sharding import Mesh, PartitionSpec as P

BW = 64
NA = 1024
PLANE = ("x", "c", "zh", "zl")
NT = (((1,), (1,)), ((), ()))
SWAP = [(0, 1), (1, 0)]
VMEM = pl.BlockSpec(memory_space=pltpu.VMEM)
HBM = pl.BlockSpec(memory_space=pltpu.HBM)
SMEM = pl.BlockSpec(memory_space=pltpu.SMEM)
PARAMS = pltpu.CompilerParams(vmem_limit_bytes=40 * 2**20)
WIDE = pltpu.CompilerParams(vmem_limit_bytes=46 * 2**20)
ALONE = pltpu.CompilerParams(vmem_limit_bytes=59 * 2**20)


def shape(*sizes, dtype=jnp.bfloat16):
    return jax.ShapeDtypeStruct(sizes, dtype)


def from_four(one, axis):
    return [one] + [lax.ppermute(one, axis, [(i, i ^ j) for i in range(4)]) for j in range(1, 4)]


def place_kernel(where, pieces0, pieces1, pieces2, pieces3, half):
    y, x, zh, zl = where[0], where[1], where[2], where[3]
    for y_step, pieces in enumerate((pieces0, pieces1, pieces2, pieces3)):
        from_y = lax.bitwise_xor(y, y_step)
        from_zl = lax.bitwise_xor(zl, from_y // 2)
        col = pl.multiple_of(from_zl * 256, 256)
        for x_step in range(4):
            from_x = lax.bitwise_xor(x, x_step)
            row_block = lax.rem(from_x, 2) * 2 + from_x // 2
            for z_step in range(2):
                from_zh = lax.bitwise_xor(zh, lax.rem(from_y, 2) * 2 + z_step)
                row = pl.multiple_of(row_block * 256 + from_zh * BW, BW)
                half[pl.ds(row, BW), pl.ds(col, 256)] = pieces[x_step, z_step]


def join_kernel(where, mine, theirs, whole, sems):
    core = where[4]
    copies = [
        pltpu.make_async_copy(
            source, whole.at[pl.ds(0, NA), pl.ds(pl.multiple_of(place * 512, 512), 512)], sems.at[index]
        )
        for index, (source, place) in enumerate(((mine, core), (theirs, 1 - core)))
    ]
    for copy in copies:
        copy.start()
    for copy in copies:
        copy.wait()


def scale_row(blocks):
    place = lax.broadcasted_iota(jnp.int32, (1, 256), 1) // BW
    row = jnp.zeros((1, 256), jnp.float32)
    for index, entry in enumerate(blocks):
        row = jnp.where(place == index, entry.astype(jnp.float32), row)
    return row


def block_kernel(mask, block, out, scalars, held, sems):
    copies = [
        pltpu.make_async_copy(mask, scalars, sems.at[0]),
        pltpu.make_async_copy(block, held, sems.at[1]),
    ]
    for copy in copies:
        copy.start()
    for copy in copies:
        copy.wait()
    row = scale_row([scalars[0, index] for index in range(4)])
    out[...] = (held[...].astype(jnp.float32) * row).astype(jnp.bfloat16)


def screen_kernel(mask, integrals, out, scalars, held, sems, out_sems):
    inward, outward = [], []
    for index in range(8):
        part = pl.ds(index * 8, 8)
        inward.append(pltpu.make_async_copy(integrals.at[part], held.at[part], sems.at[index]))
        outward.append(pltpu.make_async_copy(held.at[part], out.at[part], out_sems.at[index]))
    first = pltpu.make_async_copy(mask, scalars, sems.at[8])
    first.start()
    for copy in inward:
        copy.start()
    first.wait()
    row = scale_row([scalars[0, 0, index] for index in range(4)]).astype(jnp.bfloat16)
    for index in range(8):
        part = pl.ds(index * 8, 8)
        inward[index].wait()
        held[part] = held[part] * row[None]
        outward[index].start()
    for copy in outward:
        copy.wait()


def pick_rows(core, screened, rows):
    for x in range(4):
        for y in range(4):
            for zl in range(2):
                low = pl.multiple_of((y * 4 + zl * 2 + core) * BW + x * 16, 16)
                to = ((x * 4 + y) * 2 + zl) * 16
                rows[to : to + 16, :] = screened[pl.ds(low, 16), :]


def contract_rows(rows, density, contracted, half):
    contracted[:, half] = jnp.dot(rows[...], density[:, half], preferred_element_type=jnp.float32).astype(
        jnp.bfloat16
    )


def exchange_rows(contracted, screened, half):
    return lax.dot_general(contracted[...], screened[half, :], NT, preferred_element_type=jnp.float32)


HALVES = (slice(0, 512), slice(512, 1024))


def first_kernel(where, parts, density_in, out, screened, density, rows, contracted, sems):
    fetch = [
        pltpu.make_async_copy(
            density_in.at[pl.ds(0, NA), pl.ds(half * 512, 512)],
            density.at[:, pl.ds(half * 512, 512)],
            sems.at[half],
        )
        for half in range(2)
    ]
    for copy in fetch:
        copy.start()
    for x in range(4):
        for zh in range(4):
            low = (x * 4 + zh) * BW
            for zl in range(2):
                for core in range(2):
                    left = (core * 2 + zl) * 256
                    screened[low : low + BW, left : left + 256] = parts[((x * 2 + core) * 4 + zh) * 2 + zl]
    pick_rows(1 - where[4], screened, rows)
    for copy, half in zip(fetch, HALVES):
        copy.wait()
        contract_rows(rows, density, contracted, half)
    for half in HALVES:
        out[:, half] = exchange_rows(contracted, screened, half).astype(jnp.bfloat16)


def second_kernel(where, screened, density, out, rows, contracted):
    pick_rows(where[4], screened, rows)
    for half in HALVES:
        contract_rows(rows, density, contracted, half)
    for half in HALVES:
        out[:, half] = exchange_rows(contracted, screened, half)


def gather_z(block):
    return [
        lax.ppermute(
            block,
            ("y", "zl", "zh"),
            [(y * 8 + z, y * 8 + (z ^ (y * 2 + step))) for y in range(4) for z in range(8)],
        )
        for step in range(2)
    ]


def gather(where, two):
    plane = jnp.stack(from_four(jnp.stack(two), "x"))
    half = pl.pallas_call(
        place_kernel,
        out_shape=shape(NA, 512),
        in_specs=[SMEM] + [VMEM] * 4,
        out_specs=VMEM,
        compiler_params=PARAMS,
        cost_estimate=pl.CostEstimate(flops=0, bytes_accessed=2 * 2**20, transcendentals=0),
        name="place",
    )(where, *from_four(plane, "y"))
    return pl.pallas_call(
        join_kernel,
        out_shape=shape(8 * NA, NA),
        in_specs=[SMEM] + [VMEM] * 2,
        out_specs=HBM,
        scratch_shapes=[pltpu.SemaphoreType.DMA((2,))],
        compiler_params=PARAMS,
        cost_estimate=pl.CostEstimate(flops=0, bytes_accessed=4 * 2**20, transcendentals=0),
        name="join",
    )(where, half, lax.ppermute(half, "c", SWAP))


def body(integrals, integral_mask, density, density_mask):
    where = jnp.stack([lax.axis_index(name) for name in ("y", "x", "zh", "zl", "c")]).astype(jnp.int32)
    block = pl.pallas_call(
        block_kernel,
        out_shape=shape(BW, 256),
        in_specs=[HBM] * 2,
        out_specs=VMEM,
        scratch_shapes=[
            pltpu.SMEM((1, 4), jnp.int32),
            pltpu.VMEM((BW, 256), jnp.bfloat16),
            pltpu.SemaphoreType.DMA((2,)),
        ],
        compiler_params=ALONE,
        name="block",
    )(density_mask.T, density.T)
    screened = pl.pallas_call(
        screen_kernel,
        out_shape=shape(64, 64, 256),
        in_specs=[HBM] * 2,
        out_specs=HBM,
        scratch_shapes=[
            pltpu.SMEM((1, 1, 4), jnp.int32),
            pltpu.VMEM((64, 64, 256), jnp.bfloat16),
            pltpu.SemaphoreType.DMA((9,)),
            pltpu.SemaphoreType.DMA((8,)),
        ],
        compiler_params=ALONE,
        cost_estimate=pl.CostEstimate(flops=0, bytes_accessed=4 * 2**20, transcendentals=0),
        name="screen",
    )(integral_mask, integrals)
    two = gather_z(block)
    screened, two = lax.optimization_barrier((screened, two))
    parts = lax.all_to_all(screened, PLANE, split_axis=0, concat_axis=0, tiled=True)
    whole = gather(where, two)
    other_half, screened, whole = pl.pallas_call(
        first_kernel,
        out_shape=(shape(NA // 2, NA), shape(NA, NA), shape(NA, NA)),
        in_specs=[SMEM, VMEM, HBM],
        out_specs=(VMEM, VMEM, VMEM),
        scratch_shapes=[pltpu.VMEM((NA // 2, NA), jnp.bfloat16)] * 2 + [pltpu.SemaphoreType.DMA((2,))],
        compiler_params=WIDE,
        cost_estimate=pl.CostEstimate(flops=2**31, bytes_accessed=8 * 2**20, transcendentals=0),
        name="other",
    )(where, parts, whole)
    arrived = lax.ppermute(other_half, "c", SWAP)
    own_half = pl.pallas_call(
        second_kernel,
        out_shape=shape(NA // 2, NA, dtype=jnp.float32),
        in_specs=[SMEM] + [VMEM] * 2,
        out_specs=VMEM,
        scratch_shapes=[pltpu.VMEM((NA // 2, NA), jnp.bfloat16)] * 2,
        compiler_params=PARAMS,
        cost_estimate=pl.CostEstimate(flops=2**31, bytes_accessed=6 * 2**20, transcendentals=0),
        name="own",
    )(where, screened, whole)
    term = (own_half + arrived.astype(jnp.float32)).astype(jnp.bfloat16).reshape(16, 32, NA)
    layers = lax.all_to_all(term, ("x", "y"), split_axis=0, concat_axis=0, tiled=True)
    column = jnp.sum(layers.astype(jnp.float32), axis=0).reshape(8, 4, NA)
    terms = lax.all_to_all(column, ("zl", "zh"), split_axis=0, concat_axis=0, tiled=True)
    return jnp.sum(terms, axis=0)


def solution(mesh):
    fine = Mesh(mesh.devices.reshape(4, 2, 2, 4, 4), ("y", "zl", "c", "x", "zh"))
    m, n = ("zl", "c"), ("x", "zh")
    in_specs = (P("y", n, m), P("y", n, m), P(m, n), P(m, n))
    out_specs = P(("y", "zl", "c", "x", "zh"), None)
    return jax.shard_map(body, mesh=fine, in_specs=in_specs, out_specs=out_specs, check_vma=False)
```

```python
import jax
import jax.numpy as jnp
from jax import lax
from jax.experimental import pallas as pl
from jax.experimental.pallas import tpu as pltpu
from jax.sharding import Mesh, PartitionSpec as P

BW = 64
NA = 1024
PLANE = ("x", "c", "zh", "zl")
NT = (((1,), (1,)), ((), ()))
SWAP = [(0, 1), (1, 0)]
VMEM = pl.BlockSpec(memory_space=pltpu.VMEM)
HBM = pl.BlockSpec(memory_space=pltpu.HBM)
SMEM = pl.BlockSpec(memory_space=pltpu.SMEM)
PARAMS = pltpu.CompilerParams(vmem_limit_bytes=40 * 2**20)
WIDE = pltpu.CompilerParams(vmem_limit_bytes=46 * 2**20)
ALONE = pltpu.CompilerParams(vmem_limit_bytes=59 * 2**20)


def shape(*sizes, dtype=jnp.bfloat16):
    return jax.ShapeDtypeStruct(sizes, dtype)


def from_four(one, axis):
    return [one] + [lax.ppermute(one, axis, [(i, i ^ j) for i in range(4)]) for j in range(1, 4)]


def place_kernel(where, pieces0, pieces1, pieces2, pieces3, half):
    y, x, zh, zl = where[0], where[1], where[2], where[3]
    for y_step, pieces in enumerate((pieces0, pieces1, pieces2, pieces3)):
        from_y = lax.bitwise_xor(y, y_step)
        from_zl = lax.bitwise_xor(zl, from_y // 2)
        col = pl.multiple_of(from_zl * 256, 256)
        for x_step in range(4):
            from_x = lax.bitwise_xor(x, x_step)
            row_block = lax.rem(from_x, 2) * 2 + from_x // 2
            for z_step in range(2):
                from_zh = lax.bitwise_xor(zh, lax.rem(from_y, 2) * 2 + z_step)
                row = pl.multiple_of(row_block * 256 + from_zh * BW, BW)
                half[pl.ds(row, BW), pl.ds(col, 256)] = pieces[x_step, z_step]


def pair_kernel(first, second, out):
    out[0] = first[...]
    out[1] = second[...]


def join_kernel(where, mine, theirs, whole, sems):
    core = where[4]
    copies = [
        pltpu.make_async_copy(
            source, whole.at[pl.ds(0, NA), pl.ds(pl.multiple_of(place * 512, 512), 512)], sems.at[index]
        )
        for index, (source, place) in enumerate(((mine, core), (theirs, 1 - core)))
    ]
    for copy in copies:
        copy.start()
    for copy in copies:
        copy.wait()


def scale_row(blocks):
    place = lax.broadcasted_iota(jnp.int32, (1, 256), 1) // BW
    row = jnp.zeros((1, 256), jnp.float32)
    for index, entry in enumerate(blocks):
        row = jnp.where(place == index, entry.astype(jnp.float32), row)
    return row


def prepare_kernel(block_mask, block, mask, integrals, block_out, out, block_scalars, scalars, block_in, held, sems, out_sems):
    small = [
        pltpu.make_async_copy(block_mask, block_scalars, sems.at[0]),
        pltpu.make_async_copy(block, block_in, sems.at[1]),
        pltpu.make_async_copy(mask, scalars, sems.at[2]),
    ]
    for copy in small:
        copy.start()
    inward, outward = [], []
    for index in range(8):
        part = pl.ds(index * 8, 8)
        inward.append(pltpu.make_async_copy(integrals.at[part], held.at[part], sems.at[3 + index]))
        outward.append(pltpu.make_async_copy(held.at[part], out.at[part], out_sems.at[index]))
        inward[-1].start()
    for copy in small:
        copy.wait()
    row = scale_row([block_scalars[0, index] for index in range(4)])
    block_out[...] = (block_in[...].astype(jnp.float32) * row).astype(jnp.bfloat16)
    row = scale_row([scalars[0, 0, index] for index in range(4)]).astype(jnp.bfloat16)
    for index in range(8):
        part = pl.ds(index * 8, 8)
        inward[index].wait()
        held[part] = held[part] * row[None]
        outward[index].start()
    for copy in outward:
        copy.wait()


def pick_rows(core, screened, rows):
    for x in range(4):
        for y in range(4):
            for zl in range(2):
                to = ((x * 4 + y) * 2 + zl) * 16
                rows[to : to + 16, :] = screened[y, zl * 2 + core, x * 16 : (x + 1) * 16, :]


def contract_rows(rows, density, contracted, half):
    columns = slice(half * 512, (half + 1) * 512)
    contracted[:, columns] = jnp.dot(
        rows[...], density[:, columns], preferred_element_type=jnp.float32
    ).astype(jnp.bfloat16)


def exchange_rows(contracted, screened, half):
    several = screened[half * 2 : half * 2 + 2].reshape(512, NA)
    return lax.dot_general(contracted[...], several, NT, preferred_element_type=jnp.float32)


def first_kernel(where, parts, density_in, out, screened, density, rows, contracted, sems):
    me = where[4]
    fetch = []
    for half in range(2):
        columns = pl.ds(half * 512, 512)
        fetch.append(
            pltpu.make_async_copy(density_in.at[pl.ds(0, NA), columns], density.at[:, columns], sems.at[half])
        )
        fetch[half].start()
    for source in range(2):
        for z in range(2):
            left = (source * 2 + z) * 256
            for zh in range(4):
                screened[:, zh, :, left : left + 256] = parts[:, source, zh, z]
    pick_rows(1 - me, screened, rows)
    for half in range(2):
        fetch[half].wait()
        contract_rows(rows, density, contracted, half)
    for half in range(2):
        out[:, half * 512 : (half + 1) * 512] = exchange_rows(contracted, screened, half).astype(jnp.bfloat16)


def second_kernel(where, screened, density, out, rows, contracted):
    pick_rows(where[4], screened, rows)
    for half in range(2):
        contract_rows(rows, density, contracted, half)
    for half in range(2):
        out[:, half * 512 : (half + 1) * 512] = exchange_rows(contracted, screened, half)


def gather_z(block):
    return [
        lax.ppermute(
            block,
            ("y", "zl", "zh"),
            [(y * 8 + z, y * 8 + (z ^ (y * 2 + step))) for y in range(4) for z in range(8)],
        )
        for step in range(2)
    ]


def gather(where, two):
    pair = pl.pallas_call(
        pair_kernel,
        out_shape=shape(2, BW, 256),
        in_specs=[VMEM] * 2,
        out_specs=VMEM,
        compiler_params=PARAMS,
        cost_estimate=pl.CostEstimate(flops=2**35, bytes_accessed=2**17, transcendentals=0),
        name="pair",
    )(*two)
    plane = jnp.stack(from_four(pair, "x"))
    half = pl.pallas_call(
        place_kernel,
        out_shape=shape(NA, 512),
        in_specs=[SMEM] + [VMEM] * 4,
        out_specs=VMEM,
        compiler_params=PARAMS,
        cost_estimate=pl.CostEstimate(flops=0, bytes_accessed=2 * 2**20, transcendentals=0),
        name="place",
    )(where, *from_four(plane, "y"))
    return pl.pallas_call(
        join_kernel,
        out_shape=shape(8 * NA, NA),
        in_specs=[SMEM] + [VMEM] * 2,
        out_specs=HBM,
        scratch_shapes=[pltpu.SemaphoreType.DMA((2,))],
        compiler_params=PARAMS,
        cost_estimate=pl.CostEstimate(flops=0, bytes_accessed=4 * 2**20, transcendentals=0),
        name="join",
    )(where, half, lax.ppermute(half, "c", SWAP))


def body(integrals, integral_mask, density, density_mask):
    where = jnp.stack([lax.axis_index(name) for name in ("y", "x", "zh", "zl", "c")]).astype(jnp.int32)
    block, screened = pl.pallas_call(
        prepare_kernel,
        out_shape=(shape(BW, 256), shape(64, 64, 256)),
        in_specs=[HBM] * 4,
        out_specs=(VMEM, HBM),
        scratch_shapes=[
            pltpu.SMEM((1, 4), jnp.int32),
            pltpu.SMEM((1, 1, 4), jnp.int32),
            pltpu.VMEM((BW, 256), jnp.bfloat16),
            pltpu.VMEM((64, 64, 256), jnp.bfloat16),
            pltpu.SemaphoreType.DMA((11,)),
            pltpu.SemaphoreType.DMA((8,)),
        ],
        compiler_params=ALONE,
        cost_estimate=pl.CostEstimate(flops=0, bytes_accessed=4 * 2**20, transcendentals=0),
        name="prepare",
    )(density_mask.T, density.T, integral_mask, integrals)
    two = gather_z(block)
    parts = lax.all_to_all(screened, PLANE, split_axis=0, concat_axis=0, tiled=True)
    whole = gather(where, two)
    other_half, screened, whole = pl.pallas_call(
        first_kernel,
        out_shape=(shape(NA // 2, NA), shape(4, 4, BW, NA), shape(NA, NA)),
        in_specs=[SMEM, VMEM, HBM],
        out_specs=(VMEM, VMEM, VMEM),
        scratch_shapes=[pltpu.VMEM((NA // 2, NA), jnp.bfloat16)] * 2 + [pltpu.SemaphoreType.DMA((2,))],
        compiler_params=WIDE,
        cost_estimate=pl.CostEstimate(flops=2**31, bytes_accessed=8 * 2**20, transcendentals=0),
        name="other",
    )(where, parts.reshape(4, 2, 4, 2, BW, 256), whole)
    arrived = lax.ppermute(other_half, "c", SWAP)
    own_half = pl.pallas_call(
        second_kernel,
        out_shape=shape(NA // 2, NA, dtype=jnp.float32),
        in_specs=[SMEM] + [VMEM] * 2,
        out_specs=VMEM,
        scratch_shapes=[pltpu.VMEM((NA // 2, NA), jnp.bfloat16)] * 2,
        compiler_params=PARAMS,
        cost_estimate=pl.CostEstimate(flops=2**31, bytes_accessed=6 * 2**20, transcendentals=0),
        name="own",
    )(where, screened, whole)
    term = (own_half + arrived.astype(jnp.float32)).astype(jnp.bfloat16).reshape(16, 32, NA)
    layers = lax.all_to_all(term, ("x", "y"), split_axis=0, concat_axis=0, tiled=True)
    column = jnp.sum(layers.astype(jnp.float32), axis=0).reshape(8, 4, NA)
    terms = lax.all_to_all(column, ("zl", "zh"), split_axis=0, concat_axis=0, tiled=True)
    return jnp.sum(terms, axis=0)


def solution(mesh):
    fine = Mesh(mesh.devices.reshape(4, 2, 2, 4, 4), ("y", "zl", "c", "x", "zh"))
    m, n = ("zl", "c"), ("x", "zh")
    in_specs = (P("y", n, m), P("y", n, m), P(m, n), P(m, n))
    out_specs = P(("y", "zl", "c", "x", "zh"), None)
    return jax.shard_map(body, mesh=fine, in_specs=in_specs, out_specs=out_specs, check_vma=False)
```

```python
import jax
import jax.numpy as jnp
from jax import lax
from jax.experimental import pallas as pl
from jax.experimental.pallas import tpu as pltpu
from jax.sharding import Mesh, PartitionSpec as P

BW = 64
NA = 1024
PLANE = ("x", "c", "zh", "zl")
NT = (((1,), (1,)), ((), ()))
SWAP = [(0, 1), (1, 0)]
STEPS = (2, 1, 3, 0)
VMEM = pl.BlockSpec(memory_space=pltpu.VMEM)
HBM = pl.BlockSpec(memory_space=pltpu.HBM)
SMEM = pl.BlockSpec(memory_space=pltpu.SMEM)
PARAMS = pltpu.CompilerParams(vmem_limit_bytes=40 * 2**20)
WIDE = pltpu.CompilerParams(vmem_limit_bytes=42 * 2**20)
ALONE = pltpu.CompilerParams(vmem_limit_bytes=59 * 2**20)


def shape(*sizes, dtype=jnp.bfloat16):
    return jax.ShapeDtypeStruct(sizes, dtype)


def from_four(one, axis):
    return [one] + [lax.ppermute(one, axis, [(i, i ^ j) for i in range(4)]) for j in range(1, 4)]


def place_kernel(where, pieces0, pieces1, pieces2, pieces3, half):
    y, x, zh, zl = where[0], where[1], where[2], where[3]
    for y_step, pieces in enumerate((pieces0, pieces1, pieces2, pieces3)):
        from_y = lax.bitwise_xor(y, y_step)
        from_zl = lax.bitwise_xor(zl, from_y // 2)
        col = pl.multiple_of(from_zl * 256, 256)
        for x_step in range(4):
            from_x = lax.bitwise_xor(x, x_step)
            row_block = lax.rem(from_x, 2) * 2 + from_x // 2
            for z_step in range(2):
                from_zh = lax.bitwise_xor(zh, lax.rem(from_y, 2) * 2 + z_step)
                row = pl.multiple_of(row_block * 256 + from_zh * BW, BW)
                half[pl.ds(row, BW), pl.ds(col, 256)] = pieces[x_step, z_step]


def pair_kernel(first, second, out):
    out[0] = first[...]
    out[1] = second[...]


def join_kernel(where, mine, theirs, whole, sems):
    core = where[4]
    copies = [
        pltpu.make_async_copy(
            source, whole.at[pl.ds(0, NA), pl.ds(pl.multiple_of(place * 512, 512), 512)], sems.at[index]
        )
        for index, (source, place) in enumerate(((mine, core), (theirs, 1 - core)))
    ]
    for copy in copies:
        copy.start()
    for copy in copies:
        copy.wait()


def scale_row(blocks):
    place = lax.broadcasted_iota(jnp.int32, (1, 256), 1) // BW
    row = jnp.zeros((1, 256), jnp.float32)
    for index, entry in enumerate(blocks):
        row = jnp.where(place == index, entry.astype(jnp.float32), row)
    return row


def prepare_kernel(block_mask, block, mask, integrals, block_out, out, block_scalars, scalars, block_in, held, sems, out_sems):
    small = [
        pltpu.make_async_copy(block_mask, block_scalars, sems.at[0]),
        pltpu.make_async_copy(block, block_in, sems.at[1]),
        pltpu.make_async_copy(mask, scalars, sems.at[2]),
    ]
    for copy in small:
        copy.start()
    inward, outward = [], []
    for index in range(8):
        part = pl.ds(index * 8, 8)
        inward.append(pltpu.make_async_copy(integrals.at[part], held.at[part], sems.at[3 + index]))
        outward.append(pltpu.make_async_copy(held.at[part], out.at[part], out_sems.at[index]))
        inward[-1].start()
    for copy in small:
        copy.wait()
    row = scale_row([block_scalars[0, index] for index in range(4)])
    block_out[...] = (block_in[...].astype(jnp.float32) * row).astype(jnp.bfloat16)
    row = scale_row([scalars[0, 0, index] for index in range(4)]).astype(jnp.bfloat16)
    for index in range(8):
        part = pl.ds(index * 8, 8)
        inward[index].wait()
        held[part] = held[part] * row[None]
        outward[index].start()
    for copy in outward:
        copy.wait()


def pick_rows(where, core, screened, rows):
    for index, step in enumerate(STEPS):
        for zl in range(2):
            to = (index * 2 + zl) * BW
            rows[to : to + BW, :] = screened[lax.bitwise_xor(where[0], step), zl * 2 + core]


def contract_rows(rows, density, contracted, half):
    columns = slice(half * 512, (half + 1) * 512)
    contracted[:, columns] = jnp.dot(
        rows[...], density[:, columns], preferred_element_type=jnp.float32
    ).astype(jnp.bfloat16)


def exchange_rows(contracted, screened, half):
    several = screened[half * 2 : half * 2 + 2].reshape(512, NA)
    return lax.dot_general(contracted[...], several, NT, preferred_element_type=jnp.float32)


def first_kernel(where, parts, density_in, out, screened, density, contracted, rows, sems):
    fetch = []
    for half in range(2):
        columns = pl.ds(half * 512, 512)
        for part in range(4):
            low = pl.ds(part * 256, 256)
            fetch.append(
                pltpu.make_async_copy(
                    density_in.at[low, columns], density.at[low, columns], sems.at[half * 4 + part]
                )
            )
            fetch[-1].start()
    for source in range(2):
        for z in range(2):
            left = (source * 2 + z) * 256
            for zh in range(4):
                screened[:, zh, :, left : left + 256] = parts[:, source, zh, z]
    pick_rows(where, 1 - where[4], screened, rows)
    for half in range(2):
        for copy in fetch[half * 4 : half * 4 + 4]:
            copy.wait()
        contract_rows(rows, density, contracted, half)
    for half in range(2):
        out[:, half * 512 : (half + 1) * 512] = exchange_rows(contracted.at[:256], screened, half)


def second_kernel(where, screened, density, contracted, rows):
    pick_rows(where, where[4], screened, rows)
    for half in range(2):
        contract_rows(rows, density, contracted, half)


def rest_kernel(contracted, screened, out):
    for half in range(2):
        out[:, half * 512 : (half + 1) * 512] = exchange_rows(contracted, screened, half)


def add_kernel(first, second, third, out):
    out[...] = first[...] + second[...].astype(jnp.float32) + third[...].astype(jnp.float32)


def third_kernel(contracted, screened, arrived, out_a, out_b):
    for half in range(2):
        columns = slice(half * 512, (half + 1) * 512)
        got = exchange_rows(contracted, screened, half) + arrived[:, columns]
        out_a[:, columns] = got[:128].astype(out_a.dtype)
        out_b[:, columns] = got[128:].astype(out_b.dtype)


def gather_z(block):
    return [
        lax.ppermute(
            block,
            ("y", "zl", "zh"),
            [(y * 8 + z, y * 8 + (z ^ (y * 2 + step))) for y in range(4) for z in range(8)],
        )
        for step in range(2)
    ]


def gather(where, two):
    pair = pl.pallas_call(
        pair_kernel,
        out_shape=shape(2, BW, 256),
        in_specs=[VMEM] * 2,
        out_specs=VMEM,
        compiler_params=PARAMS,
        cost_estimate=pl.CostEstimate(flops=2**35, bytes_accessed=2**17, transcendentals=0),
        name="pair",
    )(*two)
    plane = jnp.stack(from_four(pair, "x"))
    half = pl.pallas_call(
        place_kernel,
        out_shape=shape(NA, 512),
        in_specs=[SMEM] + [VMEM] * 4,
        out_specs=VMEM,
        compiler_params=PARAMS,
        cost_estimate=pl.CostEstimate(flops=0, bytes_accessed=2 * 2**20, transcendentals=0),
        name="place",
    )(where, *from_four(plane, "y"))
    return pl.pallas_call(
        join_kernel,
        out_shape=shape(8 * NA, NA),
        in_specs=[SMEM] + [VMEM] * 2,
        out_specs=HBM,
        scratch_shapes=[pltpu.SemaphoreType.DMA((2,))],
        compiler_params=PARAMS,
        cost_estimate=pl.CostEstimate(flops=0, bytes_accessed=4 * 2**20, transcendentals=0),
        name="join",
    )(where, half, lax.ppermute(half, "c", SWAP))


def body(integrals, integral_mask, density, density_mask):
    where = jnp.stack([lax.axis_index(name) for name in ("y", "x", "zh", "zl", "c")]).astype(jnp.int32)
    block, screened = pl.pallas_call(
        prepare_kernel,
        out_shape=(shape(BW, 256), shape(64, 64, 256)),
        in_specs=[HBM] * 4,
        out_specs=(VMEM, HBM),
        scratch_shapes=[
            pltpu.SMEM((1, 4), jnp.int32),
            pltpu.SMEM((1, 1, 4), jnp.int32),
            pltpu.VMEM((BW, 256), jnp.bfloat16),
            pltpu.VMEM((64, 64, 256), jnp.bfloat16),
            pltpu.SemaphoreType.DMA((11,)),
            pltpu.SemaphoreType.DMA((8,)),
        ],
        compiler_params=ALONE,
        cost_estimate=pl.CostEstimate(flops=0, bytes_accessed=4 * 2**20, transcendentals=0),
        name="prepare",
    )(density_mask.T, density.T, integral_mask, integrals)
    two = gather_z(block)
    parts = lax.all_to_all(screened, PLANE, split_axis=0, concat_axis=0, tiled=True)
    whole = gather(where, two)
    near_out, screened, whole, far_rows = pl.pallas_call(
        first_kernel,
        out_shape=(shape(256, NA, dtype=jnp.float32), shape(4, 4, BW, NA), shape(NA, NA), shape(512, NA)),
        in_specs=[SMEM, VMEM, HBM],
        out_specs=(VMEM,) * 4,
        scratch_shapes=[pltpu.VMEM((512, NA), jnp.bfloat16), pltpu.SemaphoreType.DMA((8,))],
        compiler_params=WIDE,
        cost_estimate=pl.CostEstimate(flops=3 * 2**29, bytes_accessed=8 * 2**20, transcendentals=0),
        name="first",
    )(where, parts.reshape(4, 2, 4, 2, BW, 256), whole)
    arrived = lax.ppermute(near_out, "c", SWAP)
    contracted = pl.pallas_call(
        second_kernel,
        out_shape=shape(512, NA),
        in_specs=[SMEM] + [VMEM] * 2,
        out_specs=VMEM,
        scratch_shapes=[pltpu.VMEM((512, NA), jnp.bfloat16)],
        compiler_params=PARAMS,
        cost_estimate=pl.CostEstimate(flops=2**30, bytes_accessed=5 * 2**20, transcendentals=0),
        name="own",
    )(where, screened, whole)
    half_rows = [pl.BlockSpec((256, NA), lambda i, half=half: (half, 0)) for half in range(2)]
    everything = pl.BlockSpec((4, 4, BW, NA), lambda i: (0, 0, 0, 0))
    near = pl.pallas_call(
        third_kernel,
        out_shape=(shape(128, NA),) * 2,
        grid=(1,),
        in_specs=[half_rows[0], everything, half_rows[0]],
        out_specs=(VMEM,) * 2,
        compiler_params=PARAMS,
        cost_estimate=pl.CostEstimate(flops=2**29, bytes_accessed=4 * 2**20, transcendentals=0),
        name="near",
    )(contracted, screened, arrived)
    far_rows, near = lax.optimization_barrier((far_rows, near))
    arrived = lax.ppermute(
        pl.pallas_call(
            rest_kernel,
            out_shape=shape(256, NA, dtype=jnp.float32),
            grid=(1,),
            in_specs=[half_rows[1], everything],
            out_specs=half_rows[0],
            compiler_params=PARAMS,
            cost_estimate=pl.CostEstimate(flops=2**29, bytes_accessed=4 * 2**20, transcendentals=0),
            name="rest",
        )(far_rows, screened),
        "c",
        SWAP,
    )
    far, own = pl.pallas_call(
        third_kernel,
        out_shape=(shape(128, NA), shape(128, NA, dtype=jnp.float32)),
        grid=(1,),
        in_specs=[half_rows[1], everything, half_rows[0]],
        out_specs=(VMEM,) * 2,
        compiler_params=PARAMS,
        cost_estimate=pl.CostEstimate(flops=2**29, bytes_accessed=4 * 2**20, transcendentals=0),
        name="far",
    )(contracted, screened, arrived)
    sent = [
        lax.ppermute(quarter, "y", [(i, i ^ step) for i in range(4)])
        for step, quarter in zip(STEPS, (near[0], near[1], far))
    ]
    total = pl.pallas_call(
        add_kernel,
        out_shape=shape(128, NA, dtype=jnp.float32),
        in_specs=[VMEM] * 3,
        out_specs=VMEM,
        compiler_params=PARAMS,
        cost_estimate=pl.CostEstimate(flops=2**35, bytes_accessed=2**21, transcendentals=0),
        name="add",
    )(own, sent[0], sent[1])
    term = (total + sent[2].astype(jnp.float32)).astype(jnp.bfloat16).reshape(32, 4, NA)
    terms = lax.all_to_all(term, ("zl", "x", "zh"), split_axis=0, concat_axis=0, tiled=True)
    return jnp.sum(terms.astype(jnp.float32), axis=0)


def solution(mesh):
    fine = Mesh(mesh.devices.reshape(4, 2, 2, 4, 4), ("y", "zl", "c", "x", "zh"))
    m, n = ("zl", "c"), ("x", "zh")
    in_specs = (P("y", n, m), P("y", n, m), P(m, n), P(m, n))
    out_specs = P(("y", "zl", "c", "x", "zh"), None)
    return jax.shard_map(body, mesh=fine, in_specs=in_specs, out_specs=out_specs, check_vma=False)
```

```python
import jax
import jax.numpy as jnp
from jax import lax
from jax.experimental import pallas as pl
from jax.experimental.pallas import tpu as pltpu
from jax.sharding import Mesh, PartitionSpec as P

BW = 64
NA = 1024
PLANE = ("x", "c", "zh", "zl")
NT = (((1,), (1,)), ((), ()))
SWAP = [(0, 1), (1, 0)]
STEPS = (1, 3, 2, 0)
VMEM = pl.BlockSpec(memory_space=pltpu.VMEM)
HBM = pl.BlockSpec(memory_space=pltpu.HBM)
SMEM = pl.BlockSpec(memory_space=pltpu.SMEM)
PARAMS = pltpu.CompilerParams(vmem_limit_bytes=40 * 2**20)
WIDE = pltpu.CompilerParams(vmem_limit_bytes=42 * 2**20)
ALONE = pltpu.CompilerParams(vmem_limit_bytes=59 * 2**20)


def shape(*sizes, dtype=jnp.bfloat16):
    return jax.ShapeDtypeStruct(sizes, dtype)


def from_four(one, axis):
    return [one] + [lax.ppermute(one, axis, [(i, i ^ j) for i in range(4)]) for j in range(1, 4)]


def place_kernel(where, pieces0, pieces1, pieces2, pieces3, half):
    y, x, zh, zl = where[0], where[1], where[2], where[3]
    for y_step, pieces in enumerate((pieces0, pieces1, pieces2, pieces3)):
        from_y = lax.bitwise_xor(y, y_step)
        from_zl = lax.bitwise_xor(zl, from_y // 2)
        col = pl.multiple_of(from_zl * 256, 256)
        for x_step in range(4):
            from_x = lax.bitwise_xor(x, x_step)
            row_block = lax.rem(from_x, 2) * 2 + from_x // 2
            for z_step in range(2):
                from_zh = lax.bitwise_xor(zh, lax.rem(from_y, 2) * 2 + z_step)
                row = pl.multiple_of(row_block * 256 + from_zh * BW, BW)
                half[pl.ds(row, BW), pl.ds(col, 256)] = pieces[x_step, z_step]


def pair_kernel(first, second, out):
    out[0] = first[...]
    out[1] = second[...]


def join_kernel(where, mine, theirs, whole, sems):
    core = where[4]
    copies = [
        pltpu.make_async_copy(
            source, whole.at[pl.ds(0, NA), pl.ds(pl.multiple_of(place * 512, 512), 512)], sems.at[index]
        )
        for index, (source, place) in enumerate(((mine, core), (theirs, 1 - core)))
    ]
    for copy in copies:
        copy.start()
    for copy in copies:
        copy.wait()


def scale_row(blocks):
    place = lax.broadcasted_iota(jnp.int32, (1, 256), 1) // BW
    row = jnp.zeros((1, 256), jnp.float32)
    for index, entry in enumerate(blocks):
        row = jnp.where(place == index, entry.astype(jnp.float32), row)
    return row


def prepare_kernel(block_mask, block, mask, integrals, block_out, out, block_scalars, scalars, block_in, held, sems, out_sems):
    small = [
        pltpu.make_async_copy(block_mask, block_scalars, sems.at[0]),
        pltpu.make_async_copy(block, block_in, sems.at[1]),
        pltpu.make_async_copy(mask, scalars, sems.at[2]),
    ]
    for copy in small:
        copy.start()
    inward, outward = [], []
    for index in range(8):
        part = pl.ds(index * 8, 8)
        inward.append(pltpu.make_async_copy(integrals.at[part], held.at[part], sems.at[3 + index]))
        outward.append(pltpu.make_async_copy(held.at[part], out.at[part], out_sems.at[index]))
        inward[-1].start()
    for copy in small:
        copy.wait()
    row = scale_row([block_scalars[0, index] for index in range(4)])
    block_out[...] = (block_in[...].astype(jnp.float32) * row).astype(jnp.bfloat16)
    row = scale_row([scalars[0, 0, index] for index in range(4)]).astype(jnp.bfloat16)
    for index in range(8):
        part = pl.ds(index * 8, 8)
        inward[index].wait()
        held[part] = held[part] * row[None]
        outward[index].start()
    for copy in outward:
        copy.wait()


def pick_rows(where, core, screened, rows):
    for index, step in enumerate(STEPS):
        for zl in range(2):
            to = (index * 2 + zl) * BW
            rows[to : to + BW, :] = screened[lax.bitwise_xor(where[0], step), zl * 2 + core]


def contract_rows(rows, density, contracted, half):
    columns = slice(half * 512, (half + 1) * 512)
    contracted[:, columns] = jnp.dot(
        rows[...], density[:, columns], preferred_element_type=jnp.float32
    ).astype(jnp.bfloat16)


def exchange_rows(contracted, screened, half):
    several = screened[half * 2 : half * 2 + 2].reshape(512, NA)
    return lax.dot_general(contracted[...], several, NT, preferred_element_type=jnp.float32)


def first_kernel(where, parts, density_in, near, far, screened, density, rows, contracted, sems):
    fetch = []
    for half in range(2):
        columns = pl.ds(half * 512, 512)
        for part in range(4):
            low = pl.ds(part * 256, 256)
            fetch.append(
                pltpu.make_async_copy(
                    density_in.at[low, columns], density.at[low, columns], sems.at[half * 4 + part]
                )
            )
            fetch[-1].start()
    for source in range(2):
        for z in range(2):
            left = (source * 2 + z) * 256
            for zh in range(4):
                screened[:, zh, :, left : left + 256] = parts[:, source, zh, z]
    pick_rows(where, 1 - where[4], screened, rows)
    for half in range(2):
        for copy in fetch[half * 4 : half * 4 + 4]:
            copy.wait()
        contract_rows(rows, density, contracted, half)
    for half in range(2):
        columns = slice(half * 512, (half + 1) * 512)
        got = exchange_rows(contracted, screened, half)
        near[:, columns] = got[:256]
        far[:, columns] = got[256:]


def second_kernel(where, screened, density, contracted, rows):
    pick_rows(where, where[4], screened, rows)
    for half in range(2):
        contract_rows(rows, density, contracted, half)


def add_kernel(first, second, third, out):
    out[...] = first[...] + second[...].astype(jnp.float32) + third[...].astype(jnp.float32)


def third_kernel(contracted, screened, arrived, out_a, out_b):
    for half in range(2):
        columns = slice(half * 512, (half + 1) * 512)
        got = exchange_rows(contracted, screened, half) + arrived[:, columns]
        out_a[:, columns] = got[:128].astype(out_a.dtype)
        out_b[:, columns] = got[128:].astype(out_b.dtype)


def gather_z(block):
    return [
        lax.ppermute(
            block,
            ("y", "zl", "zh"),
            [(y * 8 + z, y * 8 + (z ^ (y * 2 + step))) for y in range(4) for z in range(8)],
        )
        for step in range(2)
    ]


def gather(where, two):
    pair = pl.pallas_call(
        pair_kernel,
        out_shape=shape(2, BW, 256),
        in_specs=[VMEM] * 2,
        out_specs=VMEM,
        compiler_params=PARAMS,
        cost_estimate=pl.CostEstimate(flops=2**35, bytes_accessed=2**17, transcendentals=0),
        name="pair",
    )(*two)
    plane = jnp.stack(from_four(pair, "x"))
    half = pl.pallas_call(
        place_kernel,
        out_shape=shape(NA, 512),
        in_specs=[SMEM] + [VMEM] * 4,
        out_specs=VMEM,
        compiler_params=PARAMS,
        cost_estimate=pl.CostEstimate(flops=0, bytes_accessed=2 * 2**20, transcendentals=0),
        name="place",
    )(where, *from_four(plane, "y"))
    return pl.pallas_call(
        join_kernel,
        out_shape=shape(8 * NA, NA),
        in_specs=[SMEM] + [VMEM] * 2,
        out_specs=HBM,
        scratch_shapes=[pltpu.SemaphoreType.DMA((2,))],
        compiler_params=PARAMS,
        cost_estimate=pl.CostEstimate(flops=0, bytes_accessed=4 * 2**20, transcendentals=0),
        name="join",
    )(where, half, lax.ppermute(half, "c", SWAP))


def body(integrals, integral_mask, density, density_mask):
    where = jnp.stack([lax.axis_index(name) for name in ("y", "x", "zh", "zl", "c")]).astype(jnp.int32)
    block, screened = pl.pallas_call(
        prepare_kernel,
        out_shape=(shape(BW, 256), shape(64, 64, 256)),
        in_specs=[HBM] * 4,
        out_specs=(VMEM, HBM),
        scratch_shapes=[
            pltpu.SMEM((1, 4), jnp.int32),
            pltpu.SMEM((1, 1, 4), jnp.int32),
            pltpu.VMEM((BW, 256), jnp.bfloat16),
            pltpu.VMEM((64, 64, 256), jnp.bfloat16),
            pltpu.SemaphoreType.DMA((11,)),
            pltpu.SemaphoreType.DMA((8,)),
        ],
        compiler_params=ALONE,
        cost_estimate=pl.CostEstimate(flops=0, bytes_accessed=4 * 2**20, transcendentals=0),
        name="prepare",
    )(density_mask.T, density.T, integral_mask, integrals)
    two = gather_z(block)
    parts = lax.all_to_all(screened, PLANE, split_axis=0, concat_axis=0, tiled=True)
    whole = gather(where, two)
    f32 = jnp.float32
    near, far, screened, whole = pl.pallas_call(
        first_kernel,
        out_shape=(shape(256, NA, dtype=f32), shape(256, NA, dtype=f32), shape(4, 4, BW, NA), shape(NA, NA)),
        in_specs=[SMEM, VMEM, HBM],
        out_specs=(VMEM,) * 4,
        scratch_shapes=[pltpu.VMEM((512, NA), jnp.bfloat16)] * 2 + [pltpu.SemaphoreType.DMA((8,))],
        compiler_params=WIDE,
        cost_estimate=pl.CostEstimate(flops=2**31, bytes_accessed=8 * 2**20, transcendentals=0),
        name="first",
    )(where, parts.reshape(4, 2, 4, 2, BW, 256), whole)
    arrived = [lax.ppermute(one, "c", SWAP) for one in (near, far)]
    contracted = pl.pallas_call(
        second_kernel,
        out_shape=shape(512, NA),
        in_specs=[SMEM] + [VMEM] * 2,
        out_specs=VMEM,
        scratch_shapes=[pltpu.VMEM((512, NA), jnp.bfloat16)],
        compiler_params=PARAMS,
        cost_estimate=pl.CostEstimate(flops=2**30, bytes_accessed=5 * 2**20, transcendentals=0),
        name="own",
    )(where, screened, whole)
    half_rows = [pl.BlockSpec((256, NA), lambda i, half=half: (half, 0)) for half in range(2)]
    everything = pl.BlockSpec((4, 4, BW, NA), lambda i: (0, 0, 0, 0))
    near = pl.pallas_call(
        third_kernel,
        out_shape=(shape(128, NA),) * 2,
        grid=(1,),
        in_specs=[half_rows[0], everything, half_rows[0]],
        out_specs=(VMEM,) * 2,
        compiler_params=PARAMS,
        cost_estimate=pl.CostEstimate(flops=2**29, bytes_accessed=4 * 2**20, transcendentals=0),
        name="near",
    )(contracted, screened, arrived[0])
    contracted, near = lax.optimization_barrier((contracted, near))
    far, own = pl.pallas_call(
        third_kernel,
        out_shape=(shape(128, NA), shape(128, NA, dtype=jnp.float32)),
        grid=(1,),
        in_specs=[half_rows[1], everything, half_rows[0]],
        out_specs=(VMEM,) * 2,
        compiler_params=PARAMS,
        cost_estimate=pl.CostEstimate(flops=2**29, bytes_accessed=4 * 2**20, transcendentals=0),
        name="far",
    )(contracted, screened, arrived[1])
    sent = [
        lax.ppermute(quarter, "y", [(i, i ^ step) for i in range(4)])
        for step, quarter in zip(STEPS, (near[0], near[1], far))
    ]
    total = pl.pallas_call(
        add_kernel,
        out_shape=shape(128, NA, dtype=jnp.float32),
        in_specs=[VMEM] * 3,
        out_specs=VMEM,
        compiler_params=PARAMS,
        cost_estimate=pl.CostEstimate(flops=2**35, bytes_accessed=2**21, transcendentals=0),
        name="add",
    )(own, sent[0], sent[1])
    term = (total + sent[2].astype(jnp.float32)).astype(jnp.bfloat16).reshape(32, 4, NA)
    terms = lax.all_to_all(term, ("zl", "x", "zh"), split_axis=0, concat_axis=0, tiled=True)
    return jnp.sum(terms.astype(jnp.float32), axis=0)


def solution(mesh):
    fine = Mesh(mesh.devices.reshape(4, 2, 2, 4, 4), ("y", "zl", "c", "x", "zh"))
    m, n = ("zl", "c"), ("x", "zh")
    in_specs = (P("y", n, m), P("y", n, m), P(m, n), P(m, n))
    out_specs = P(("y", "zl", "c", "x", "zh"), None)
    return jax.shard_map(body, mesh=fine, in_specs=in_specs, out_specs=out_specs, check_vma=False)
```

```python
import jax
import jax.numpy as jnp
from jax import lax
from jax.experimental import pallas as pl
from jax.experimental.pallas import tpu as pltpu
from jax.sharding import Mesh, PartitionSpec as P

BW = 64
NA = 1024
PLANE = ("x", "c", "zh", "zl")
NT = (((1,), (1,)), ((), ()))
SWAP = [(0, 1), (1, 0)]
STEPS = (1, 3, 2, 0)
VMEM = pl.BlockSpec(memory_space=pltpu.VMEM)
HBM = pl.BlockSpec(memory_space=pltpu.HBM)
SMEM = pl.BlockSpec(memory_space=pltpu.SMEM)
PARAMS = pltpu.CompilerParams(vmem_limit_bytes=40 * 2**20)
WIDE = pltpu.CompilerParams(vmem_limit_bytes=42 * 2**20)
ALONE = pltpu.CompilerParams(vmem_limit_bytes=59 * 2**20)


def shape(*sizes, dtype=jnp.bfloat16):
    return jax.ShapeDtypeStruct(sizes, dtype)


def from_four(one, axis):
    return [one] + [lax.ppermute(one, axis, [(i, i ^ j) for i in range(4)]) for j in range(1, 4)]


def place_kernel(where, pieces0, pieces1, pieces2, pieces3, half):
    y, x, zh, zl = where[0], where[1], where[2], where[3]
    for y_step, pieces in enumerate((pieces0, pieces1, pieces2, pieces3)):
        from_y = lax.bitwise_xor(y, y_step)
        from_zl = lax.bitwise_xor(zl, from_y // 2)
        col = pl.multiple_of(from_zl * 256, 256)
        for x_step in range(4):
            from_x = lax.bitwise_xor(x, x_step)
            row_block = lax.rem(from_x, 2) * 2 + from_x // 2
            for z_step in range(2):
                from_zh = lax.bitwise_xor(zh, lax.rem(from_y, 2) * 2 + z_step)
                row = pl.multiple_of(row_block * 256 + from_zh * BW, BW)
                half[pl.ds(row, BW), pl.ds(col, 256)] = pieces[x_step, z_step]


def pair_kernel(first, second, out):
    out[0] = first[...]
    out[1] = second[...]


def join_kernel(where, mine, theirs, whole, sems):
    core = where[4]
    copies = [
        pltpu.make_async_copy(
            source, whole.at[pl.ds(0, NA), pl.ds(pl.multiple_of(place * 512, 512), 512)], sems.at[index]
        )
        for index, (source, place) in enumerate(((mine, core), (theirs, 1 - core)))
    ]
    for copy in copies:
        copy.start()
    for copy in copies:
        copy.wait()


def scale_row(blocks):
    place = lax.broadcasted_iota(jnp.int32, (1, 256), 1) // BW
    row = jnp.zeros((1, 256), jnp.float32)
    for index, entry in enumerate(blocks):
        row = jnp.where(place == index, entry.astype(jnp.float32), row)
    return row


def prepare_kernel(block_mask, block, mask, integrals, block_out, out, block_scalars, scalars, block_in, held, sems, out_sems):
    small = [
        pltpu.make_async_copy(block_mask, block_scalars, sems.at[0]),
        pltpu.make_async_copy(block, block_in, sems.at[1]),
        pltpu.make_async_copy(mask, scalars, sems.at[2]),
    ]
    for copy in small:
        copy.start()
    inward, outward = [], []
    for index in range(8):
        part = pl.ds(index * 8, 8)
        inward.append(pltpu.make_async_copy(integrals.at[part], held.at[part], sems.at[3 + index]))
        outward.append(pltpu.make_async_copy(held.at[part], out.at[part], out_sems.at[index]))
        inward[-1].start()
    for copy in small:
        copy.wait()
    row = scale_row([block_scalars[0, index] for index in range(4)])
    block_out[...] = (block_in[...].astype(jnp.float32) * row).astype(jnp.bfloat16)
    row = scale_row([scalars[0, 0, index] for index in range(4)]).astype(jnp.bfloat16)
    for index in range(8):
        part = pl.ds(index * 8, 8)
        inward[index].wait()
        held[part] = held[part] * row[None]
        outward[index].start()
    for copy in outward:
        copy.wait()


def pick_rows(where, core, screened, rows):
    for index, step in enumerate(STEPS):
        for zl in range(2):
            to = (index * 2 + zl) * BW
            rows[to : to + BW, :] = screened[lax.bitwise_xor(where[0], step), zl * 2 + core]


def contract_rows(rows, density, contracted, half):
    columns = slice(half * 512, (half + 1) * 512)
    contracted[:, columns] = jnp.dot(
        rows[...], density[:, columns], preferred_element_type=jnp.float32
    ).astype(jnp.bfloat16)


def exchange_rows(contracted, screened, half):
    several = screened[half * 2 : half * 2 + 2].reshape(512, NA)
    return lax.dot_general(contracted[...], several, NT, preferred_element_type=jnp.float32)


def first_kernel(where, parts, density_in, near, far, screened, density, own_rows, rows, contracted, sems):
    fetch = []
    for half in range(2):
        columns = pl.ds(half * 512, 512)
        for part in range(4):
            low = pl.ds(part * 256, 256)
            fetch.append(
                pltpu.make_async_copy(
                    density_in.at[low, columns], density.at[low, columns], sems.at[half * 4 + part]
                )
            )
            fetch[-1].start()
    for source in range(2):
        for z in range(2):
            left = (source * 2 + z) * 256
            for zh in range(4):
                screened[:, zh, :, left : left + 256] = parts[:, source, zh, z]
    pick_rows(where, 1 - where[4], screened, rows)
    pick_rows(where, where[4], screened, own_rows)
    for half in range(2):
        for copy in fetch[half * 4 : half * 4 + 4]:
            copy.wait()
        contract_rows(rows, density, contracted, half)
    for half in range(2):
        columns = slice(half * 512, (half + 1) * 512)
        got = exchange_rows(contracted, screened, half)
        near[:, columns] = got[:256].astype(near.dtype)
        far[:, columns] = got[256:]


def second_kernel(rows, density, contracted):
    for half in range(2):
        contract_rows(rows, density, contracted, half)


def add_kernel(first, second, third, out):
    out[...] = first[...] + second[...].astype(jnp.float32) + third[...].astype(jnp.float32)


def third_kernel(contracted, screened, arrived, out_a, out_b):
    for half in range(2):
        columns = slice(half * 512, (half + 1) * 512)
        got = exchange_rows(contracted, screened, half) + arrived[:, columns].astype(jnp.float32)
        out_a[:, columns] = got[:128].astype(out_a.dtype)
        out_b[:, columns] = got[128:].astype(out_b.dtype)


def gather_z(block):
    return [
        lax.ppermute(
            block,
            ("y", "zl", "zh"),
            [(y * 8 + z, y * 8 + (z ^ (y * 2 + step))) for y in range(4) for z in range(8)],
        )
        for step in range(2)
    ]


def gather(where, two):
    pair = pl.pallas_call(
        pair_kernel,
        out_shape=shape(2, BW, 256),
        in_specs=[VMEM] * 2,
        out_specs=VMEM,
        compiler_params=PARAMS,
        cost_estimate=pl.CostEstimate(flops=2**35, bytes_accessed=2**17, transcendentals=0),
        name="pair",
    )(*two)
    plane = jnp.stack(from_four(pair, "x"))
    half = pl.pallas_call(
        place_kernel,
        out_shape=shape(NA, 512),
        in_specs=[SMEM] + [VMEM] * 4,
        out_specs=VMEM,
        compiler_params=PARAMS,
        cost_estimate=pl.CostEstimate(flops=0, bytes_accessed=2 * 2**20, transcendentals=0),
        name="place",
    )(where, *from_four(plane, "y"))
    return pl.pallas_call(
        join_kernel,
        out_shape=shape(8 * NA, NA),
        in_specs=[SMEM] + [VMEM] * 2,
        out_specs=HBM,
        scratch_shapes=[pltpu.SemaphoreType.DMA((2,))],
        compiler_params=PARAMS,
        cost_estimate=pl.CostEstimate(flops=0, bytes_accessed=4 * 2**20, transcendentals=0),
        name="join",
    )(where, half, lax.ppermute(half, "c", SWAP))


def body(integrals, integral_mask, density, density_mask):
    where = jnp.stack([lax.axis_index(name) for name in ("y", "x", "zh", "zl", "c")]).astype(jnp.int32)
    block, screened = pl.pallas_call(
        prepare_kernel,
        out_shape=(shape(BW, 256), shape(64, 64, 256)),
        in_specs=[HBM] * 4,
        out_specs=(VMEM, HBM),
        scratch_shapes=[
            pltpu.SMEM((1, 4), jnp.int32),
            pltpu.SMEM((1, 1, 4), jnp.int32),
            pltpu.VMEM((BW, 256), jnp.bfloat16),
            pltpu.VMEM((64, 64, 256), jnp.bfloat16),
            pltpu.SemaphoreType.DMA((11,)),
            pltpu.SemaphoreType.DMA((8,)),
        ],
        compiler_params=ALONE,
        cost_estimate=pl.CostEstimate(flops=0, bytes_accessed=4 * 2**20, transcendentals=0),
        name="prepare",
    )(density_mask.T, density.T, integral_mask, integrals)
    two = gather_z(block)
    parts = lax.all_to_all(screened, PLANE, split_axis=0, concat_axis=0, tiled=True)
    whole = gather(where, two)
    f32 = jnp.float32
    near, far, screened, whole, rows = pl.pallas_call(
        first_kernel,
        out_shape=(shape(256, NA), shape(256, NA, dtype=f32), shape(4, 4, BW, NA), shape(NA, NA), shape(512, NA)),
        in_specs=[SMEM, VMEM, HBM],
        out_specs=(VMEM,) * 5,
        scratch_shapes=[pltpu.VMEM((512, NA), jnp.bfloat16)] * 2 + [pltpu.SemaphoreType.DMA((8,))],
        compiler_params=WIDE,
        cost_estimate=pl.CostEstimate(flops=2**31, bytes_accessed=8 * 2**20, transcendentals=0),
        name="first",
    )(where, parts.reshape(4, 2, 4, 2, BW, 256), whole)
    arrived = lax.ppermute(near, "c", SWAP)
    contracted = pl.pallas_call(
        second_kernel,
        out_shape=shape(512, NA),
        in_specs=[VMEM] * 2,
        out_specs=VMEM,
        compiler_params=PARAMS,
        cost_estimate=pl.CostEstimate(flops=2**30, bytes_accessed=5 * 2**20, transcendentals=0),
        name="own",
    )(rows, whole)
    half_rows = [pl.BlockSpec((256, NA), lambda i, half=half: (half, 0)) for half in range(2)]
    everything = pl.BlockSpec((4, 4, BW, NA), lambda i: (0, 0, 0, 0))
    near = pl.pallas_call(
        third_kernel,
        out_shape=(shape(128, NA),) * 2,
        grid=(1,),
        in_specs=[half_rows[0], everything, half_rows[0]],
        out_specs=(VMEM,) * 2,
        compiler_params=PARAMS,
        cost_estimate=pl.CostEstimate(flops=2**29, bytes_accessed=4 * 2**20, transcendentals=0),
        name="near",
    )(contracted, screened, arrived)
    contracted, far, near = lax.optimization_barrier((contracted, far, near))
    far, own = pl.pallas_call(
        third_kernel,
        out_shape=(shape(128, NA), shape(128, NA, dtype=jnp.float32)),
        grid=(1,),
        in_specs=[half_rows[1], everything, half_rows[0]],
        out_specs=(VMEM,) * 2,
        compiler_params=PARAMS,
        cost_estimate=pl.CostEstimate(flops=2**29, bytes_accessed=4 * 2**20, transcendentals=0),
        name="far",
    )(contracted, screened, lax.ppermute(far, "c", SWAP))
    sent = [
        lax.ppermute(quarter, "y", [(i, i ^ step) for i in range(4)])
        for step, quarter in zip(STEPS, (near[0], near[1], far))
    ]
    total = pl.pallas_call(
        add_kernel,
        out_shape=shape(128, NA, dtype=jnp.float32),
        in_specs=[VMEM] * 3,
        out_specs=VMEM,
        compiler_params=PARAMS,
        cost_estimate=pl.CostEstimate(flops=2**35, bytes_accessed=2**21, transcendentals=0),
        name="add",
    )(own, sent[0], sent[1])
    term = (total + sent[2].astype(jnp.float32)).astype(jnp.bfloat16).reshape(32, 4, NA)
    terms = lax.all_to_all(term, ("zl", "x", "zh"), split_axis=0, concat_axis=0, tiled=True)
    return jnp.sum(terms.astype(jnp.float32), axis=0)


def solution(mesh):
    fine = Mesh(mesh.devices.reshape(4, 2, 2, 4, 4), ("y", "zl", "c", "x", "zh"))
    m, n = ("zl", "c"), ("x", "zh")
    in_specs = (P("y", n, m), P("y", n, m), P(m, n), P(m, n))
    out_specs = P(("y", "zl", "c", "x", "zh"), None)
    return jax.shard_map(body, mesh=fine, in_specs=in_specs, out_specs=out_specs, check_vma=False)
```

```python
import jax
import jax.numpy as jnp
from jax import lax
from jax.experimental import pallas as pl
from jax.experimental.pallas import tpu as pltpu
from jax.sharding import Mesh, PartitionSpec as P

BW = 64
NA = 1024
PLANE = ("x", "c", "zh", "zl")
NT = (((1,), (1,)), ((), ()))
SWAP = [(0, 1), (1, 0)]
STEPS = (1, 3, 2, 0)
VMEM = pl.BlockSpec(memory_space=pltpu.VMEM)
HBM = pl.BlockSpec(memory_space=pltpu.HBM)
SMEM = pl.BlockSpec(memory_space=pltpu.SMEM)
PARAMS = pltpu.CompilerParams(vmem_limit_bytes=40 * 2**20)
WIDE = pltpu.CompilerParams(vmem_limit_bytes=42 * 2**20)
ALONE = pltpu.CompilerParams(vmem_limit_bytes=59 * 2**20)


def shape(*sizes, dtype=jnp.bfloat16):
    return jax.ShapeDtypeStruct(sizes, dtype)


def from_four(one, axis):
    return [one] + [lax.ppermute(one, axis, [(i, i ^ j) for i in range(4)]) for j in range(1, 4)]


def place_kernel(where, pieces0, pieces1, pieces2, pieces3, half):
    y, x, zh, zl = where[0], where[1], where[2], where[3]
    for y_step, pieces in enumerate((pieces0, pieces1, pieces2, pieces3)):
        from_y = lax.bitwise_xor(y, y_step)
        from_zl = lax.bitwise_xor(zl, from_y // 2)
        col = pl.multiple_of(from_zl * 256, 256)
        for x_step in range(4):
            from_x = lax.bitwise_xor(x, x_step)
            row_block = lax.rem(from_x, 2) * 2 + from_x // 2
            for z_step in range(2):
                from_zh = lax.bitwise_xor(zh, lax.rem(from_y, 2) * 2 + z_step)
                row = pl.multiple_of(row_block * 256 + from_zh * BW, BW)
                half[pl.ds(row, BW), pl.ds(col, 256)] = pieces[x_step, z_step]


def pair_kernel(first, second, out):
    out[0] = first[...]
    out[1] = second[...]


def join_kernel(where, mine, theirs, whole, sems):
    core = where[4]
    copies = [
        pltpu.make_async_copy(
            source, whole.at[pl.ds(0, NA), pl.ds(pl.multiple_of(place * 512, 512), 512)], sems.at[index]
        )
        for index, (source, place) in enumerate(((mine, core), (theirs, 1 - core)))
    ]
    for copy in copies:
        copy.start()
    for copy in copies:
        copy.wait()


def scale_row(blocks):
    place = lax.broadcasted_iota(jnp.int32, (1, 256), 1) // BW
    row = jnp.zeros((1, 256), jnp.float32)
    for index, entry in enumerate(blocks):
        row = jnp.where(place == index, entry.astype(jnp.float32), row)
    return row


def prepare_kernel(block_mask, block, mask, integrals, block_out, out, block_scalars, scalars, block_in, held, sems, out_sems):
    small = [
        pltpu.make_async_copy(block_mask, block_scalars, sems.at[0]),
        pltpu.make_async_copy(block, block_in, sems.at[1]),
        pltpu.make_async_copy(mask, scalars, sems.at[2]),
    ]
    for copy in small:
        copy.start()
    inward, outward = [], []
    for index in range(8):
        part = pl.ds(index * 8, 8)
        inward.append(pltpu.make_async_copy(integrals.at[part], held.at[part], sems.at[3 + index]))
        outward.append(pltpu.make_async_copy(held.at[part], out.at[part], out_sems.at[index]))
        inward[-1].start()
    for copy in small:
        copy.wait()
    row = scale_row([block_scalars[0, index] for index in range(4)])
    block_out[...] = (block_in[...].astype(jnp.float32) * row).astype(jnp.bfloat16)
    row = scale_row([scalars[0, 0, index] for index in range(4)]).astype(jnp.bfloat16)
    for index in range(8):
        part = pl.ds(index * 8, 8)
        inward[index].wait()
        held[part] = held[part] * row[None]
        outward[index].start()
    for copy in outward:
        copy.wait()


def pick_rows(where, core, screened, rows):
    for index, step in enumerate(STEPS):
        for zl in range(2):
            to = (index * 2 + zl) * BW
            rows[to : to + BW, :] = screened[lax.bitwise_xor(where[0], step), zl * 2 + core]


def contract_rows(rows, density, contracted, half):
    columns = slice(half * 512, (half + 1) * 512)
    contracted[:, columns] = jnp.dot(
        rows[...], density[:, columns], preferred_element_type=jnp.float32
    ).astype(jnp.bfloat16)


def exchange_rows(contracted, screened, half):
    several = screened[half * 2 : half * 2 + 2].reshape(512, NA)
    return lax.dot_general(contracted[...], several, NT, preferred_element_type=jnp.float32)


def first_kernel(where, parts, density_in, near, later, screened, density, own_rows, rows, contracted, sems):
    fetch = []
    for half in range(2):
        columns = pl.ds(half * 512, 512)
        for part in range(4):
            low = pl.ds(part * 256, 256)
            fetch.append(
                pltpu.make_async_copy(
                    density_in.at[low, columns], density.at[low, columns], sems.at[half * 4 + part]
                )
            )
            fetch[-1].start()
    for source in range(2):
        for z in range(2):
            left = (source * 2 + z) * 256
            for zh in range(4):
                screened[:, zh, :, left : left + 256] = parts[:, source, zh, z]
    pick_rows(where, 1 - where[4], screened, rows)
    pick_rows(where, where[4], screened, own_rows)
    for half in range(2):
        for copy in fetch[half * 4 : half * 4 + 4]:
            copy.wait()
        contract_rows(rows, density, contracted, half)
    for half in range(2):
        columns = slice(half * 512, (half + 1) * 512)
        near[:, columns] = exchange_rows(contracted.at[:256], screened, half).astype(near.dtype)
    later[...] = contracted[256:, :]


def second_kernel(rows, density, later, screened, contracted, far):
    for half in range(2):
        contract_rows(rows, density, contracted, half)
    for half in range(2):
        far[:, half * 512 : (half + 1) * 512] = exchange_rows(later, screened, half)


def add_kernel(first, second, third, out):
    out[...] = first[...] + second[...].astype(jnp.float32) + third[...].astype(jnp.float32)


def third_kernel(contracted, screened, arrived, out_a, out_b):
    for half in range(2):
        columns = slice(half * 512, (half + 1) * 512)
        got = exchange_rows(contracted, screened, half) + arrived[:, columns].astype(jnp.float32)
        out_a[:, columns] = got[:128].astype(out_a.dtype)
        out_b[:, columns] = got[128:].astype(out_b.dtype)


def gather_z(block):
    return [
        lax.ppermute(
            block,
            ("y", "zl", "zh"),
            [(y * 8 + z, y * 8 + (z ^ (y * 2 + step))) for y in range(4) for z in range(8)],
        )
        for step in range(2)
    ]


def gather(where, two):
    pair = pl.pallas_call(
        pair_kernel,
        out_shape=shape(2, BW, 256),
        in_specs=[VMEM] * 2,
        out_specs=VMEM,
        compiler_params=PARAMS,
        cost_estimate=pl.CostEstimate(flops=2**35, bytes_accessed=2**17, transcendentals=0),
        name="pair",
    )(*two)
    plane = jnp.stack(from_four(pair, "x"))
    half = pl.pallas_call(
        place_kernel,
        out_shape=shape(NA, 512),
        in_specs=[SMEM] + [VMEM] * 4,
        out_specs=VMEM,
        compiler_params=PARAMS,
        cost_estimate=pl.CostEstimate(flops=0, bytes_accessed=2 * 2**20, transcendentals=0),
        name="place",
    )(where, *from_four(plane, "y"))
    return pl.pallas_call(
        join_kernel,
        out_shape=shape(8 * NA, NA),
        in_specs=[SMEM] + [VMEM] * 2,
        out_specs=HBM,
        scratch_shapes=[pltpu.SemaphoreType.DMA((2,))],
        compiler_params=PARAMS,
        cost_estimate=pl.CostEstimate(flops=0, bytes_accessed=4 * 2**20, transcendentals=0),
        name="join",
    )(where, half, lax.ppermute(half, "c", SWAP))


def body(integrals, integral_mask, density, density_mask):
    where = jnp.stack([lax.axis_index(name) for name in ("y", "x", "zh", "zl", "c")]).astype(jnp.int32)
    block, screened = pl.pallas_call(
        prepare_kernel,
        out_shape=(shape(BW, 256), shape(64, 64, 256)),
        in_specs=[HBM] * 4,
        out_specs=(VMEM, HBM),
        scratch_shapes=[
            pltpu.SMEM((1, 4), jnp.int32),
            pltpu.SMEM((1, 1, 4), jnp.int32),
            pltpu.VMEM((BW, 256), jnp.bfloat16),
            pltpu.VMEM((64, 64, 256), jnp.bfloat16),
            pltpu.SemaphoreType.DMA((11,)),
            pltpu.SemaphoreType.DMA((8,)),
        ],
        compiler_params=ALONE,
        cost_estimate=pl.CostEstimate(flops=0, bytes_accessed=4 * 2**20, transcendentals=0),
        name="prepare",
    )(density_mask.T, density.T, integral_mask, integrals)
    two = gather_z(block)
    parts = lax.all_to_all(screened, PLANE, split_axis=0, concat_axis=0, tiled=True)
    whole = gather(where, two)
    f32 = jnp.float32
    near, later, screened, whole, rows = pl.pallas_call(
        first_kernel,
        out_shape=(shape(256, NA), shape(256, NA), shape(4, 4, BW, NA), shape(NA, NA), shape(512, NA)),
        in_specs=[SMEM, VMEM, HBM],
        out_specs=(VMEM,) * 5,
        scratch_shapes=[pltpu.VMEM((512, NA), jnp.bfloat16)] * 2 + [pltpu.SemaphoreType.DMA((8,))],
        compiler_params=WIDE,
        cost_estimate=pl.CostEstimate(flops=2**31, bytes_accessed=8 * 2**20, transcendentals=0),
        name="first",
    )(where, parts.reshape(4, 2, 4, 2, BW, 256), whole)
    arrived = lax.ppermute(near, "c", SWAP)
    contracted, far = pl.pallas_call(
        second_kernel,
        out_shape=(shape(512, NA), shape(256, NA, dtype=f32)),
        in_specs=[VMEM] * 4,
        out_specs=(VMEM,) * 2,
        compiler_params=PARAMS,
        cost_estimate=pl.CostEstimate(flops=3 * 2**29, bytes_accessed=8 * 2**20, transcendentals=0),
        name="own",
    )(rows, whole, later, screened)
    half_rows = [pl.BlockSpec((256, NA), lambda i, half=half: (half, 0)) for half in range(2)]
    everything = pl.BlockSpec((4, 4, BW, NA), lambda i: (0, 0, 0, 0))
    near = pl.pallas_call(
        third_kernel,
        out_shape=(shape(128, NA),) * 2,
        grid=(1,),
        in_specs=[half_rows[0], everything, half_rows[0]],
        out_specs=(VMEM,) * 2,
        compiler_params=PARAMS,
        cost_estimate=pl.CostEstimate(flops=2**29, bytes_accessed=4 * 2**20, transcendentals=0),
        name="near",
    )(contracted, screened, arrived)
    contracted, far, near = lax.optimization_barrier((contracted, far, near))
    far, own = pl.pallas_call(
        third_kernel,
        out_shape=(shape(128, NA), shape(128, NA, dtype=jnp.float32)),
        grid=(1,),
        in_specs=[half_rows[1], everything, half_rows[0]],
        out_specs=(VMEM,) * 2,
        compiler_params=PARAMS,
        cost_estimate=pl.CostEstimate(flops=2**29, bytes_accessed=4 * 2**20, transcendentals=0),
        name="far",
    )(contracted, screened, lax.ppermute(far, "c", SWAP))
    sent = [
        lax.ppermute(quarter, "y", [(i, i ^ step) for i in range(4)])
        for step, quarter in zip(STEPS, (near[0], near[1], far))
    ]
    total = pl.pallas_call(
        add_kernel,
        out_shape=shape(128, NA, dtype=jnp.float32),
        in_specs=[VMEM] * 3,
        out_specs=VMEM,
        compiler_params=PARAMS,
        cost_estimate=pl.CostEstimate(flops=2**35, bytes_accessed=2**21, transcendentals=0),
        name="add",
    )(own, sent[0], sent[1])
    term = (total + sent[2].astype(jnp.float32)).astype(jnp.bfloat16).reshape(32, 4, NA)
    terms = lax.all_to_all(term, ("zl", "x", "zh"), split_axis=0, concat_axis=0, tiled=True)
    return jnp.sum(terms.astype(jnp.float32), axis=0)


def solution(mesh):
    fine = Mesh(mesh.devices.reshape(4, 2, 2, 4, 4), ("y", "zl", "c", "x", "zh"))
    m, n = ("zl", "c"), ("x", "zh")
    in_specs = (P("y", n, m), P("y", n, m), P(m, n), P(m, n))
    out_specs = P(("y", "zl", "c", "x", "zh"), None)
    return jax.shard_map(body, mesh=fine, in_specs=in_specs, out_specs=out_specs, check_vma=False)
```

```python
import jax
import jax.numpy as jnp
from jax import lax
from jax.experimental import pallas as pl
from jax.experimental.pallas import tpu as pltpu
from jax.sharding import Mesh, PartitionSpec as P

BW = 64
NA = 1024
PLANE = ("x", "c", "zh", "zl")
NT = (((1,), (1,)), ((), ()))
SWAP = [(0, 1), (1, 0)]
STEPS = (1, 3, 2, 0)
VMEM = pl.BlockSpec(memory_space=pltpu.VMEM)
HBM = pl.BlockSpec(memory_space=pltpu.HBM)
SMEM = pl.BlockSpec(memory_space=pltpu.SMEM)
PARAMS = pltpu.CompilerParams(vmem_limit_bytes=40 * 2**20)
WIDE = pltpu.CompilerParams(vmem_limit_bytes=42 * 2**20)
ALONE = pltpu.CompilerParams(vmem_limit_bytes=59 * 2**20)


def shape(*sizes, dtype=jnp.bfloat16):
    return jax.ShapeDtypeStruct(sizes, dtype)


def from_four(one, axis):
    return [one] + [lax.ppermute(one, axis, [(i, i ^ j) for i in range(4)]) for j in range(1, 4)]


def place_kernel(where, pieces0, pieces1, pieces2, pieces3, half):
    y, x, zh, zl = where[0], where[1], where[2], where[3]
    for y_step, pieces in enumerate((pieces0, pieces1, pieces2, pieces3)):
        from_y = lax.bitwise_xor(y, y_step)
        from_zl = lax.bitwise_xor(zl, from_y // 2)
        col = pl.multiple_of(from_zl * 256, 256)
        for x_step in range(4):
            from_x = lax.bitwise_xor(x, x_step)
            row_block = lax.rem(from_x, 2) * 2 + from_x // 2
            for z_step in range(2):
                from_zh = lax.bitwise_xor(zh, lax.rem(from_y, 2) * 2 + z_step)
                row = pl.multiple_of(row_block * 256 + from_zh * BW, BW)
                half[pl.ds(row, BW), pl.ds(col, 256)] = pieces[x_step, z_step]


def pair_kernel(first, second, out):
    out[0] = first[...]
    out[1] = second[...]


def join_kernel(where, mine, theirs, whole, sems):
    core = where[4]
    copies = [
        pltpu.make_async_copy(
            source, whole.at[pl.ds(0, NA), pl.ds(pl.multiple_of(place * 512, 512), 512)], sems.at[index]
        )
        for index, (source, place) in enumerate(((mine, core), (theirs, 1 - core)))
    ]
    for copy in copies:
        copy.start()
    for copy in copies:
        copy.wait()


def scale_row(blocks):
    place = lax.broadcasted_iota(jnp.int32, (1, 256), 1) // BW
    row = jnp.zeros((1, 256), jnp.float32)
    for index, entry in enumerate(blocks):
        row = jnp.where(place == index, entry.astype(jnp.float32), row)
    return row


def prepare_kernel(block_mask, block, mask, integrals, block_out, out, block_scalars, scalars, block_in, held, sems, out_sems):
    small = [
        pltpu.make_async_copy(block_mask, block_scalars, sems.at[0]),
        pltpu.make_async_copy(block, block_in, sems.at[1]),
        pltpu.make_async_copy(mask, scalars, sems.at[2]),
    ]
    small[2].start()
    inward, outward = [], []
    for index in range(8):
        part = pl.ds(index * 8, 8)
        inward.append(pltpu.make_async_copy(integrals.at[part], held.at[part], sems.at[3 + index]))
        outward.append(pltpu.make_async_copy(held.at[part], out.at[part], out_sems.at[index]))
        inward[-1].start()
    for copy in small[:2]:
        copy.start()
    small[2].wait()
    row = scale_row([scalars[0, 0, index] for index in range(4)]).astype(jnp.bfloat16)
    for index in range(8):
        part = pl.ds(index * 8, 8)
        inward[index].wait()
        held[part] = held[part] * row[None]
        outward[index].start()
    for copy in small[:2]:
        copy.wait()
    row = scale_row([block_scalars[0, index] for index in range(4)])
    block_out[...] = (block_in[...].astype(jnp.float32) * row).astype(jnp.bfloat16)
    for copy in outward:
        copy.wait()


def pick_rows(where, core, screened, rows):
    for index, step in enumerate(STEPS):
        for zl in range(2):
            to = (index * 2 + zl) * BW
            rows[to : to + BW, :] = screened[lax.bitwise_xor(where[0], step), zl * 2 + core]


def contract_rows(rows, density, contracted, half):
    columns = slice(half * 512, (half + 1) * 512)
    contracted[:, columns] = jnp.dot(
        rows[...], density[:, columns], preferred_element_type=jnp.float32
    ).astype(jnp.bfloat16)


def exchange_rows(contracted, screened, half):
    several = screened[half * 2 : half * 2 + 2].reshape(512, NA)
    return lax.dot_general(contracted[...], several, NT, preferred_element_type=jnp.float32)


def first_kernel(where, parts, density_in, near, later, screened, density, own_rows, rows, contracted, sems):
    fetch = []
    for half in range(2):
        columns = pl.ds(half * 512, 512)
        for part in range(4):
            low = pl.ds(part * 256, 256)
            fetch.append(
                pltpu.make_async_copy(
                    density_in.at[low, columns], density.at[low, columns], sems.at[half * 4 + part]
                )
            )
            fetch[-1].start()
    for source in range(2):
        for z in range(2):
            left = (source * 2 + z) * 256
            for zh in range(4):
                screened[:, zh, :, left : left + 256] = parts[:, source, zh, z]
    pick_rows(where, 1 - where[4], screened, rows)
    pick_rows(where, where[4], screened, own_rows)
    for half in range(2):
        for copy in fetch[half * 4 : half * 4 + 4]:
            copy.wait()
        contract_rows(rows, density, contracted, half)
    for half in range(2):
        columns = slice(half * 512, (half + 1) * 512)
        near[:, columns] = exchange_rows(contracted.at[:256], screened, half).astype(near.dtype)
    later[...] = contracted[256:, :]


def second_kernel(rows, density, later, screened, contracted, far):
    for half in range(2):
        contract_rows(rows, density, contracted, half)
    for half in range(2):
        far[:, half * 512 : (half + 1) * 512] = exchange_rows(later, screened, half)


def add_kernel(first, second, third, out):
    out[...] = first[...] + second[...].astype(jnp.float32) + third[...].astype(jnp.float32)


def third_kernel(contracted, screened, arrived, out_a, out_b):
    for half in range(2):
        columns = slice(half * 512, (half + 1) * 512)
        got = exchange_rows(contracted, screened, half) + arrived[:, columns].astype(jnp.float32)
        out_a[:, columns] = got[:128].astype(out_a.dtype)
        out_b[:, columns] = got[128:].astype(out_b.dtype)


def gather_z(block):
    return [
        lax.ppermute(
            block,
            ("y", "zl", "zh"),
            [(y * 8 + z, y * 8 + (z ^ (y * 2 + step))) for y in range(4) for z in range(8)],
        )
        for step in range(2)
    ]


def gather(where, two):
    pair = pl.pallas_call(
        pair_kernel,
        out_shape=shape(2, BW, 256),
        in_specs=[VMEM] * 2,
        out_specs=VMEM,
        compiler_params=PARAMS,
        cost_estimate=pl.CostEstimate(flops=2**35, bytes_accessed=2**17, transcendentals=0),
        name="pair",
    )(*two)
    plane = jnp.stack(from_four(pair, "x"))
    half = pl.pallas_call(
        place_kernel,
        out_shape=shape(NA, 512),
        in_specs=[SMEM] + [VMEM] * 4,
        out_specs=VMEM,
        compiler_params=PARAMS,
        cost_estimate=pl.CostEstimate(flops=0, bytes_accessed=2 * 2**20, transcendentals=0),
        name="place",
    )(where, *from_four(plane, "y"))
    return pl.pallas_call(
        join_kernel,
        out_shape=shape(8 * NA, NA),
        in_specs=[SMEM] + [VMEM] * 2,
        out_specs=HBM,
        scratch_shapes=[pltpu.SemaphoreType.DMA((2,))],
        compiler_params=PARAMS,
        cost_estimate=pl.CostEstimate(flops=0, bytes_accessed=4 * 2**20, transcendentals=0),
        name="join",
    )(where, half, lax.ppermute(half, "c", SWAP))


def body(integrals, integral_mask, density, density_mask):
    where = jnp.stack([lax.axis_index(name) for name in ("y", "x", "zh", "zl", "c")]).astype(jnp.int32)
    block, screened = pl.pallas_call(
        prepare_kernel,
        out_shape=(shape(BW, 256), shape(64, 64, 256)),
        in_specs=[HBM] * 4,
        out_specs=(VMEM, HBM),
        scratch_shapes=[
            pltpu.SMEM((1, 4), jnp.int32),
            pltpu.SMEM((1, 1, 4), jnp.int32),
            pltpu.VMEM((BW, 256), jnp.bfloat16),
            pltpu.VMEM((64, 64, 256), jnp.bfloat16),
            pltpu.SemaphoreType.DMA((11,)),
            pltpu.SemaphoreType.DMA((8,)),
        ],
        compiler_params=ALONE,
        cost_estimate=pl.CostEstimate(flops=0, bytes_accessed=4 * 2**20, transcendentals=0),
        name="prepare",
    )(density_mask.T, density.T, integral_mask, integrals)
    two = gather_z(block)
    parts = lax.all_to_all(screened, PLANE, split_axis=0, concat_axis=0, tiled=True)
    whole = gather(where, two)
    f32 = jnp.float32
    near, later, screened, whole, rows = pl.pallas_call(
        first_kernel,
        out_shape=(shape(256, NA), shape(256, NA), shape(4, 4, BW, NA), shape(NA, NA), shape(512, NA)),
        in_specs=[SMEM, VMEM, HBM],
        out_specs=(VMEM,) * 5,
        scratch_shapes=[pltpu.VMEM((512, NA), jnp.bfloat16)] * 2 + [pltpu.SemaphoreType.DMA((8,))],
        compiler_params=WIDE,
        cost_estimate=pl.CostEstimate(flops=2**31, bytes_accessed=8 * 2**20, transcendentals=0),
        name="first",
    )(where, parts.reshape(4, 2, 4, 2, BW, 256), whole)
    arrived = lax.ppermute(near, "c", SWAP)
    contracted, far = pl.pallas_call(
        second_kernel,
        out_shape=(shape(512, NA), shape(256, NA, dtype=f32)),
        in_specs=[VMEM] * 4,
        out_specs=(VMEM,) * 2,
        compiler_params=PARAMS,
        cost_estimate=pl.CostEstimate(flops=3 * 2**29, bytes_accessed=8 * 2**20, transcendentals=0),
        name="own",
    )(rows, whole, later, screened)
    half_rows = [pl.BlockSpec((256, NA), lambda i, half=half: (half, 0)) for half in range(2)]
    everything = pl.BlockSpec((4, 4, BW, NA), lambda i: (0, 0, 0, 0))
    near = pl.pallas_call(
        third_kernel,
        out_shape=(shape(128, NA),) * 2,
        grid=(1,),
        in_specs=[half_rows[0], everything, half_rows[0]],
        out_specs=(VMEM,) * 2,
        compiler_params=PARAMS,
        cost_estimate=pl.CostEstimate(flops=2**29, bytes_accessed=4 * 2**20, transcendentals=0),
        name="near",
    )(contracted, screened, arrived)
    contracted, far, near = lax.optimization_barrier((contracted, far, near))
    far, own = pl.pallas_call(
        third_kernel,
        out_shape=(shape(128, NA), shape(128, NA, dtype=jnp.float32)),
        grid=(1,),
        in_specs=[half_rows[1], everything, half_rows[0]],
        out_specs=(VMEM,) * 2,
        compiler_params=PARAMS,
        cost_estimate=pl.CostEstimate(flops=2**29, bytes_accessed=4 * 2**20, transcendentals=0),
        name="far",
    )(contracted, screened, lax.ppermute(far, "c", SWAP))
    sent = [
        lax.ppermute(quarter, "y", [(i, i ^ step) for i in range(4)])
        for step, quarter in zip(STEPS, (near[0], near[1], far))
    ]
    total = pl.pallas_call(
        add_kernel,
        out_shape=shape(128, NA, dtype=jnp.float32),
        in_specs=[VMEM] * 3,
        out_specs=VMEM,
        compiler_params=PARAMS,
        cost_estimate=pl.CostEstimate(flops=2**35, bytes_accessed=2**21, transcendentals=0),
        name="add",
    )(own, sent[0], sent[1])
    term = (total + sent[2].astype(jnp.float32)).astype(jnp.bfloat16).reshape(32, 4, NA)
    terms = lax.all_to_all(term, ("zl", "x", "zh"), split_axis=0, concat_axis=0, tiled=True)
    return jnp.sum(terms.astype(jnp.float32), axis=0)


def solution(mesh):
    fine = Mesh(mesh.devices.reshape(4, 2, 2, 4, 4), ("y", "zl", "c", "x", "zh"))
    m, n = ("zl", "c"), ("x", "zh")
    in_specs = (P("y", n, m), P("y", n, m), P(m, n), P(m, n))
    out_specs = P(("y", "zl", "c", "x", "zh"), None)
    return jax.shard_map(body, mesh=fine, in_specs=in_specs, out_specs=out_specs, check_vma=False)
```

```python
import jax
import jax.numpy as jnp
from jax import lax
from jax.experimental import pallas as pl
from jax.experimental.pallas import tpu as pltpu
from jax.sharding import Mesh, PartitionSpec as P

BW = 64
NA = 1024
PLANE = ("x", "c", "zh", "zl")
NT = (((1,), (1,)), ((), ()))
SWAP = [(0, 1), (1, 0)]
STEPS = (2, 3, 1, 0)
VMEM = pl.BlockSpec(memory_space=pltpu.VMEM)
HBM = pl.BlockSpec(memory_space=pltpu.HBM)
SMEM = pl.BlockSpec(memory_space=pltpu.SMEM)
PARAMS = pltpu.CompilerParams(vmem_limit_bytes=40 * 2**20)
WIDE = pltpu.CompilerParams(vmem_limit_bytes=42 * 2**20)
ALONE = pltpu.CompilerParams(vmem_limit_bytes=59 * 2**20)


def shape(*sizes, dtype=jnp.bfloat16):
    return jax.ShapeDtypeStruct(sizes, dtype)


def from_four(one, axis):
    return [one] + [lax.ppermute(one, axis, [(i, i ^ j) for i in range(4)]) for j in range(1, 4)]


def place_kernel(where, pieces0, pieces1, pieces2, pieces3, half):
    y, x, zh, zl = where[0], where[1], where[2], where[3]
    for y_step, pieces in enumerate((pieces0, pieces1, pieces2, pieces3)):
        from_y = lax.bitwise_xor(y, y_step)
        from_zl = lax.bitwise_xor(zl, from_y // 2)
        col = pl.multiple_of(from_zl * 256, 256)
        for x_step in range(4):
            from_x = lax.bitwise_xor(x, x_step)
            row_block = lax.rem(from_x, 2) * 2 + from_x // 2
            for z_step in range(2):
                from_zh = lax.bitwise_xor(zh, lax.rem(from_y, 2) * 2 + z_step)
                row = pl.multiple_of(row_block * 256 + from_zh * BW, BW)
                half[pl.ds(row, BW), pl.ds(col, 256)] = pieces[x_step, z_step]


def pair_kernel(first, second, out):
    out[0] = first[...]
    out[1] = second[...]


def join_kernel(where, mine, theirs, whole, sems):
    core = where[4]
    copies = [
        pltpu.make_async_copy(
            source, whole.at[pl.ds(0, NA), pl.ds(pl.multiple_of(place * 512, 512), 512)], sems.at[index]
        )
        for index, (source, place) in enumerate(((mine, core), (theirs, 1 - core)))
    ]
    for copy in copies:
        copy.start()
    for copy in copies:
        copy.wait()


def scale_row(blocks):
    place = lax.broadcasted_iota(jnp.int32, (1, 256), 1) // BW
    row = jnp.zeros((1, 256), jnp.float32)
    for index, entry in enumerate(blocks):
        row = jnp.where(place == index, entry.astype(jnp.float32), row)
    return row


def prepare_kernel(block_mask, block, mask, integrals, block_out, out, block_scalars, scalars, block_in, held, sems, out_sems):
    small = [
        pltpu.make_async_copy(block_mask, block_scalars, sems.at[0]),
        pltpu.make_async_copy(block, block_in, sems.at[1]),
        pltpu.make_async_copy(mask, scalars, sems.at[2]),
    ]
    small[2].start()
    inward, outward = [], []
    for index in range(8):
        part = pl.ds(index * 8, 8)
        inward.append(pltpu.make_async_copy(integrals.at[part], held.at[part], sems.at[3 + index]))
        outward.append(pltpu.make_async_copy(held.at[part], out.at[part], out_sems.at[index]))
        inward[-1].start()
    for copy in small[:2]:
        copy.start()
    small[2].wait()
    row = scale_row([scalars[0, 0, index] for index in range(4)]).astype(jnp.bfloat16)
    for index in range(8):
        part = pl.ds(index * 8, 8)
        inward[index].wait()
        held[part] = held[part] * row[None]
        outward[index].start()
    for copy in small[:2]:
        copy.wait()
    row = scale_row([block_scalars[0, index] for index in range(4)])
    block_out[...] = (block_in[...].astype(jnp.float32) * row).astype(jnp.bfloat16)
    for copy in outward:
        copy.wait()


def pick_rows(where, core, screened, rows):
    for index, step in enumerate(STEPS):
        for zl in range(2):
            to = (index * 2 + zl) * BW
            rows[to : to + BW, :] = screened[lax.bitwise_xor(where[0], step), zl * 2 + core]


def contract_rows(rows, density, contracted, half):
    columns = slice(half * 512, (half + 1) * 512)
    contracted[:, columns] = jnp.dot(
        rows[...], density[:, columns], preferred_element_type=jnp.float32
    ).astype(jnp.bfloat16)


def exchange_rows(contracted, screened, half):
    several = screened[half * 2 : half * 2 + 2].reshape(512, NA)
    return lax.dot_general(contracted[...], several, NT, preferred_element_type=jnp.float32)


def first_kernel(where, parts, density_in, near, later, screened, density, own_rows, rows, contracted, sems):
    fetch = []
    for half in range(2):
        columns = pl.ds(half * 512, 512)
        for part in range(4):
            low = pl.ds(part * 256, 256)
            fetch.append(
                pltpu.make_async_copy(
                    density_in.at[low, columns], density.at[low, columns], sems.at[half * 4 + part]
                )
            )
            fetch[-1].start()
    for source in range(2):
        for z in range(2):
            left = (source * 2 + z) * 256
            for zh in range(4):
                screened[:, zh, :, left : left + 256] = parts[:, source, zh, z]
    pick_rows(where, 1 - where[4], screened, rows)
    pick_rows(where, where[4], screened, own_rows)
    for half in range(2):
        for copy in fetch[half * 4 : half * 4 + 4]:
            copy.wait()
        contract_rows(rows, density, contracted, half)
    for half in range(2):
        columns = slice(half * 512, (half + 1) * 512)
        near[:, columns] = exchange_rows(contracted.at[:256], screened, half).astype(near.dtype)
    later[...] = contracted[256:, :]


def second_kernel(rows, density, later, screened, contracted, far):
    for half in range(2):
        contract_rows(rows, density, contracted, half)
    for half in range(2):
        far[:, half * 512 : (half + 1) * 512] = exchange_rows(later, screened, half)


def add_kernel(first, second, third, out):
    out[...] = first[...] + second[...].astype(jnp.float32) + third[...].astype(jnp.float32)


def third_kernel(contracted, screened, arrived, out_a, out_b):
    for half in range(2):
        columns = slice(half * 512, (half + 1) * 512)
        got = exchange_rows(contracted, screened, half) + arrived[:, columns].astype(jnp.float32)
        out_a[:, columns] = got[:128].astype(out_a.dtype)
        out_b[:, columns] = got[128:].astype(out_b.dtype)


def gather_z(block):
    return [
        lax.ppermute(
            block,
            ("y", "zl", "zh"),
            [(y * 8 + z, y * 8 + (z ^ (y * 2 + step))) for y in range(4) for z in range(8)],
        )
        for step in range(2)
    ]


def gather(where, two):
    pair = pl.pallas_call(
        pair_kernel,
        out_shape=shape(2, BW, 256),
        in_specs=[VMEM] * 2,
        out_specs=VMEM,
        compiler_params=PARAMS,
        cost_estimate=pl.CostEstimate(flops=2**35, bytes_accessed=2**17, transcendentals=0),
        name="pair",
    )(*two)
    plane = jnp.stack(from_four(pair, "x"))
    half = pl.pallas_call(
        place_kernel,
        out_shape=shape(NA, 512),
        in_specs=[SMEM] + [VMEM] * 4,
        out_specs=VMEM,
        compiler_params=PARAMS,
        cost_estimate=pl.CostEstimate(flops=0, bytes_accessed=2 * 2**20, transcendentals=0),
        name="place",
    )(where, *from_four(plane, "y"))
    return pl.pallas_call(
        join_kernel,
        out_shape=shape(8 * NA, NA),
        in_specs=[SMEM] + [VMEM] * 2,
        out_specs=HBM,
        scratch_shapes=[pltpu.SemaphoreType.DMA((2,))],
        compiler_params=PARAMS,
        cost_estimate=pl.CostEstimate(flops=0, bytes_accessed=4 * 2**20, transcendentals=0),
        name="join",
    )(where, half, lax.ppermute(half, "c", SWAP))


def body(integrals, integral_mask, density, density_mask):
    where = jnp.stack([lax.axis_index(name) for name in ("y", "x", "zh", "zl", "c")]).astype(jnp.int32)
    block, screened = pl.pallas_call(
        prepare_kernel,
        out_shape=(shape(BW, 256), shape(64, 64, 256)),
        in_specs=[HBM] * 4,
        out_specs=(VMEM, HBM),
        scratch_shapes=[
            pltpu.SMEM((1, 4), jnp.int32),
            pltpu.SMEM((1, 1, 4), jnp.int32),
            pltpu.VMEM((BW, 256), jnp.bfloat16),
            pltpu.VMEM((64, 64, 256), jnp.bfloat16),
            pltpu.SemaphoreType.DMA((11,)),
            pltpu.SemaphoreType.DMA((8,)),
        ],
        compiler_params=ALONE,
        cost_estimate=pl.CostEstimate(flops=0, bytes_accessed=4 * 2**20, transcendentals=0),
        name="prepare",
    )(density_mask.T, density.T, integral_mask, integrals)
    two = gather_z(block)
    parts = lax.all_to_all(screened, PLANE, split_axis=0, concat_axis=0, tiled=True)
    whole = gather(where, two)
    f32 = jnp.float32
    near, later, screened, whole, rows = pl.pallas_call(
        first_kernel,
        out_shape=(shape(256, NA), shape(256, NA), shape(4, 4, BW, NA), shape(NA, NA), shape(512, NA)),
        in_specs=[SMEM, VMEM, HBM],
        out_specs=(VMEM,) * 5,
        scratch_shapes=[pltpu.VMEM((512, NA), jnp.bfloat16)] * 2 + [pltpu.SemaphoreType.DMA((8,))],
        compiler_params=WIDE,
        cost_estimate=pl.CostEstimate(flops=2**31, bytes_accessed=8 * 2**20, transcendentals=0),
        name="first",
    )(where, parts.reshape(4, 2, 4, 2, BW, 256), whole)
    arrived = lax.ppermute(near, "c", SWAP)
    contracted, far = pl.pallas_call(
        second_kernel,
        out_shape=(shape(512, NA), shape(256, NA, dtype=f32)),
        in_specs=[VMEM] * 4,
        out_specs=(VMEM,) * 2,
        compiler_params=PARAMS,
        cost_estimate=pl.CostEstimate(flops=3 * 2**29, bytes_accessed=8 * 2**20, transcendentals=0),
        name="own",
    )(rows, whole, later, screened)
    half_rows = [pl.BlockSpec((256, NA), lambda i, half=half: (half, 0)) for half in range(2)]
    everything = pl.BlockSpec((4, 4, BW, NA), lambda i: (0, 0, 0, 0))
    near = pl.pallas_call(
        third_kernel,
        out_shape=(shape(128, NA),) * 2,
        grid=(1,),
        in_specs=[half_rows[0], everything, half_rows[0]],
        out_specs=(VMEM,) * 2,
        compiler_params=PARAMS,
        cost_estimate=pl.CostEstimate(flops=2**29, bytes_accessed=4 * 2**20, transcendentals=0),
        name="near",
    )(contracted, screened, arrived)
    contracted, far, near = lax.optimization_barrier((contracted, far, near))
    far, own = pl.pallas_call(
        third_kernel,
        out_shape=(shape(128, NA), shape(128, NA, dtype=jnp.float32)),
        grid=(1,),
        in_specs=[half_rows[1], everything, half_rows[0]],
        out_specs=(VMEM,) * 2,
        compiler_params=PARAMS,
        cost_estimate=pl.CostEstimate(flops=2**29, bytes_accessed=4 * 2**20, transcendentals=0),
        name="far",
    )(contracted, screened, lax.ppermute(far, "c", SWAP))
    sent = [
        lax.ppermute(quarter, "y", [(i, i ^ step) for i in range(4)])
        for step, quarter in zip(STEPS, (near[0], near[1], far))
    ]
    total = pl.pallas_call(
        add_kernel,
        out_shape=shape(128, NA, dtype=jnp.float32),
        in_specs=[VMEM] * 3,
        out_specs=VMEM,
        compiler_params=PARAMS,
        cost_estimate=pl.CostEstimate(flops=2**35, bytes_accessed=2**21, transcendentals=0),
        name="add",
    )(own, sent[0], sent[1])
    term = (total + sent[2].astype(jnp.float32)).astype(jnp.bfloat16).reshape(32, 4, NA)
    terms = lax.all_to_all(term, ("zl", "x", "zh"), split_axis=0, concat_axis=0, tiled=True)
    return jnp.sum(terms.astype(jnp.float32), axis=0)


def solution(mesh):
    fine = Mesh(mesh.devices.reshape(4, 2, 2, 4, 4), ("y", "zl", "c", "x", "zh"))
    m, n = ("zl", "c"), ("x", "zh")
    in_specs = (P("y", n, m), P("y", n, m), P(m, n), P(m, n))
    out_specs = P(("y", "zl", "c", "x", "zh"), None)
    return jax.shard_map(body, mesh=fine, in_specs=in_specs, out_specs=out_specs, check_vma=False)
```
